128 devices in a mesh: row: 8 (over y, core), col: 16 (over x, z).
Axes of the slice: x: 4, y: 4, z: 4, core: 2. Of those that a mesh axis runs over, the one named last changes fastest.
Arguments:
- zvecs: float32 [8, 16, 48, 128, 128], P('row', 'col'), may hold values from -0.046875 to 0.046875
- coef: float32 [8, 16, 128, 128], P('row', 'col'), may hold values from 0.5 to 8
- blocks: float32 [8, 16, 8, 640, 640], P('row', 'col'), may hold values from -10 to 10
- send_idx: int32 [8, 16, 8, 640], P('row', 'col'), may hold values from 0 to 16383
- land_idx: int32 [8, 16, 8, 640], P('row', 'col'), may hold values from 0 to 16383
- active: int32 [8, 16, 8], P('row', 'col'), may hold values 0 or 1
- order: int32 [128], replicated, may hold values from 0 to 127, each once
Outputs:
- coarse: float32 [6144, 6144], P('row', 'col')
The draws below stay inside these ranges and needn't reach their ends.
All inputs are finite; a program needn't handle non-finite values. No bound on the sum of `active` on one device may be relied on, other than what follows from the above.
Results may differ from the reference program's by a relative error of at most 0.0003.
Values sent between devices are 32-bit elements; how exact they have to be, the bound alone decides.
A program may use at most 128 MiB of HBM per device.

```python
import math
import jax
import jax.numpy as jnp
from jax import lax

K = 48
CX = 128
CY = 128
PROWS = 640
SUBDOMAINS = 128
N_ROW = 8
N_COL = 16


def set_ends(values, rng, smallest, top_value):
    shape = values.shape
    place = [jax.random.randint(jax.random.fold_in(rng, axis), (), 0, shape[axis]) for axis in range(len(shape))]
    values = values.at[tuple(place)].set(smallest)
    longest = shape.index(max(shape))
    place[longest] = (place[longest] + 1) % shape[longest]
    return values.at[tuple(place)].set(top_value)


def level_of(stream_key, extent, shards, smallest, high):
    def one(position, blocks):
        heights = jax.random.uniform(jax.random.fold_in(jax.random.fold_in(stream_key, 6), position), (blocks,), jnp.float32, smallest / len(shards), high / len(shards))
        return jnp.repeat(jnp.exp(heights), extent[position] // blocks).reshape((-1,) + (1,) * (len(extent) - position - 1))

    gain = one(*shards[0])
    for cut in shards[1:]:
        gain = gain * one(*cut)
    return gain


def gaussian(own_key, dims, scale, bound, split=(), kind=jnp.bfloat16):
    factor_of = level_of(own_key, dims, split, -0.22, 0.18) if split else 1.0
    values = jax.random.normal(own_key, dims, jnp.float32) * scale * factor_of
    return jnp.minimum(jnp.maximum(values, -bound), bound).astype(kind)


def setup_inputs(seed: int = 0) -> dict:
    streams_of = jax.random.split(jax.random.key(seed), 8)
    return {
        "zvecs": gaussian(streams_of[0], (N_ROW, N_COL, K, CX, CY), (CX * CY) ** -0.5, 0.046875, ((0, 8), (1, 16)), jnp.float32),
        "coef": jnp.clip(jnp.exp(math.log(8.0) - 2.7725887 * jax.random.uniform(streams_of[1], (N_ROW, N_COL, CX, CY), jnp.float32) ** level_of(streams_of[1], (N_ROW, N_COL, CX, CY), ((0, 8), (1, 16)), -0.2, 0.2)), 0.5, 8.0),
        "blocks": gaussian(streams_of[2], (N_ROW, N_COL, 8, PROWS, PROWS), 2.0, 10.0, ((0, 8), (1, 16)), jnp.float32),
        "send_idx": set_ends(jax.random.randint(streams_of[3], (N_ROW, N_COL, 8, PROWS), 0, CX * CY), jax.random.fold_in(streams_of[3], 1), 0, (CX * CY) - 1).astype(jnp.int32),
        "land_idx": set_ends(jax.random.randint(streams_of[4], (N_ROW, N_COL, 8, PROWS), 0, CX * CY), jax.random.fold_in(streams_of[4], 1), 0, (CX * CY) - 1).astype(jnp.int32),
        "active": set_ends((jax.random.randint(streams_of[5], (N_ROW, N_COL, 8), 0, 4) < 3).astype(jnp.int32), jax.random.fold_in(streams_of[5], 1), 0, 1),
        "order": jax.random.permutation(streams_of[6], SUBDOMAINS).astype(jnp.int32),
    }


offsets_row = (-1, -1, -1, 0, 0, 1, 1, 1)
offsets_col = (-1, 0, 1, -1, 1, -1, 0, 1)


def local_image(zvec, coef):
    padded = jnp.pad(zvec, ((0, 0), (1, 1), (1, 1)))
    beside = padded[:, 2:, 1:-1] + padded[:, :-2, 1:-1] + padded[:, 1:-1, 2:] + padded[:, 1:-1, :-2]
    return (4.0 + coef) * zvec - beside


def reference(zvecs, coef, blocks, send_idx, land_idx, active, order):
    total = N_ROW * N_COL
    cells = CX * CY
    zflat = zvecs.reshape(total, K, cells)
    zgrid = zvecs.reshape(total, K, CX, CY)
    coefs = coef.reshape(total, CX, CY)
    blocks_f = blocks.reshape(total, 8, PROWS, PROWS)
    send_f = send_idx.reshape(total, 8, PROWS)
    land_f = land_idx.reshape(total, 8, PROWS)
    active_f = active.reshape(total, 8)
    step_row = jnp.array(offsets_row, jnp.int32)
    step_col = jnp.array(offsets_col, jnp.int32)
    everyone = jnp.arange(total, dtype=jnp.int32)

    def send_one(index):
        grid_row = index // N_COL
        grid_col = index % N_COL
        to_row = grid_row + step_row
        to_col = grid_col + step_col
        inside = (to_row >= 0) & (to_row < N_ROW) & (to_col >= 0) & (to_col < N_COL)
        keep = (inside & (active_f[index] == 1)).astype(jnp.float32)
        picked = jnp.take(zflat[index], send_f[index], axis=1)
        sent = jnp.einsum("knp,npq->nkq", picked, blocks_f[index], precision=lax.Precision.HIGHEST)
        return sent * keep[:, None, None]

    sent_all = lax.map(send_one, everyone)

    def row_one(index):
        grid_row = index // N_COL
        grid_col = index % N_COL
        from_row = grid_row - step_row
        from_col = grid_col - step_col
        inside = (from_row >= 0) & (from_row < N_ROW) & (from_col >= 0) & (from_col < N_COL)
        source = jnp.clip(from_row * N_COL + from_col, 0, total - 1).astype(jnp.int32)
        arrived = sent_all[source, jnp.arange(8, dtype=jnp.int32)]
        landed = jnp.take(zflat[index], land_f[index], axis=1)
        pair = jnp.einsum("knp,nlp->nkl", landed, arrived, precision=lax.Precision.HIGHEST)
        pair = pair * inside.astype(jnp.float32)[:, None, None]
        image = local_image(zgrid[index], coefs[index])
        own = jnp.einsum("kxy,lxy->kl", zgrid[index], image, precision=lax.Precision.HIGHEST)
        allblocks = jnp.concatenate([own[None], pair], axis=0)
        qids = jnp.concatenate([order[index][None], jnp.where(inside, order[source], -1)]).astype(jnp.int32)
        select = (qids[:, None] == everyone[None, :]).astype(jnp.float32)
        strip = jnp.einsum("bq,bkl->kql", select, allblocks, precision=lax.Precision.HIGHEST)
        return strip.reshape(K, total * K)

    rows = lax.map(row_one, everyone)
    return rows.reshape(total * K, total * K)
```

```python
import functools

import jax
import jax.numpy as jnp
from jax import lax
from jax.experimental import pallas as pl
from jax.experimental.pallas import tpu as pltpu
from jax.sharding import PartitionSpec as P

f32 = jnp.float32
bf16 = jnp.bfloat16
MESH = pl.DeviceIdType.MESH

K = 48
CX = 128
ROWS = 640
NROW = 8
NCOL = 16
NX = 4
NZ = 4
PITCH = 136
CHUNKS = 4
PER = CX // CHUNKS
HALF = K // 2
WIDE = 8 * K
STEPS = ((-1, 1), (-1, -1), (0, 1), (0, -1), (1, 1), (1, -1), (-1, 0), (1, 0))
GROUPS = ((0, 3, (0, 1)), (3, 2, (6, 7)), (5, 2, (2, 3)), (7, 2, (4, 5)))
EMPTY = NX * 9


def split(x):
    high = x.astype(bf16)
    return high, (x - high.astype(f32)).astype(bf16)


def stacked(x):
    return jnp.concatenate(split(x), axis=0)


def unstack(product):
    return product[:K, :K] + product[K : 2 * K, :K] + product[:K, K : 2 * K]


def pair_step(t, odd):
    last = t // 3
    side = 1 - last
    dr = (t - 1) * side - last + 2 * last * odd
    dc = side - 2 * side * odd
    nine = (dr + 1) * 3 + dc + 1
    return dr, dc, nine - nine // 5


def gather_rows(cells, index, start, rows):
    for j in range(ROWS):
        rows[pl.ds(j, 1), :] = cells[pl.ds(index[start + j], 1), :]


def flipped(rows):
    return rows[...].astype(bf16).T[0 : 2 * K]


def times_block(rows, block, factor, out):
    picked = flipped(rows)
    for q0 in range(0, ROWS, 256):
        q1 = min(q0 + 256, ROWS)
        total, low_total = None, None
        for p0 in range(0, ROWS, 256):
            p1 = min(p0 + 256, ROWS)
            high, low = split(block[p0:p1, q0:q1])
            one = jnp.dot(picked[:, p0:p1], high, preferred_element_type=f32)
            two = jnp.dot(picked[0:K, p0:p1], low, preferred_element_type=f32)
            total = one if total is None else total + one
            low_total = two if low_total is None else low_total + two
        out[:, q0:q1] = (total[0:K] + total[K : 2 * K] + low_total) * factor


def assemble(
    remote,
    z_hbm, coef, blocks_hbm, send_hbm, land_hbm, active, order,
    strips_out, mask_out,
    zpad, cells, blocks, rows_a, rows_b, landed, sent, arrived, held, strips, received, pick_vec,
    send_idx, land_idx, pick,
    z_sem, block_sem, send_idx_sem, land_idx_sem, pick_sem,
    near_send, near_recv, x_send, x_recv, z_send, z_recv,
):
    row = lax.axis_index("row") if remote else 3
    col = lax.axis_index("col") if remote else 5
    x_me = col // NZ
    z_me = lax.rem(col, NZ)

    if remote:
        barrier = pltpu.get_barrier_semaphore()
        for dr, dc in STEPS:
            peer = (lax.rem(row + dr + NROW, NROW), lax.rem(col + dc + NCOL, NCOL))
            pl.semaphore_signal(barrier, inc=1, device_id=peer, device_id_type=MESH)
        for k in range(1, 4):
            peer = (row, lax.rem(col + NZ * k, NCOL))
            pl.semaphore_signal(barrier, inc=1, device_id=peer, device_id_type=MESH)
            peer = (row, x_me * NZ + lax.rem(z_me + k, NZ))
            pl.semaphore_signal(barrier, inc=1, device_id=peer, device_id_type=MESH)

    z_copies = [
        pltpu.make_async_copy(
            z_hbm.at[0, 0, :, pl.ds(i * PER, PER), :],
            zpad.at[pl.ds(0, K), pl.ds(8 + i * PER, PER), :],
            z_sem.at[i],
        )
        for i in range(CHUNKS)
    ]
    for copy in z_copies:
        copy.start()
    send_copies = [
        pltpu.make_async_copy(
            send_hbm.at[0, 0, n], send_idx.at[pl.ds(n * ROWS, ROWS)], send_idx_sem.at[n]
        )
        for n in range(8)
    ]
    for copy in send_copies:
        copy.start()
    block_copies = []
    for i, (dr, dc) in enumerate(STEPS):
        nine = (dr + 1) * 3 + dc + 1
        block_copies.append(
            pltpu.make_async_copy(
                blocks_hbm.at[0, 0, nine - nine // 5], blocks.at[i], block_sem.at[i]
            )
        )
        block_copies[-1].start()
    land_copies = [
        pltpu.make_async_copy(
            land_hbm.at[0, 0, n], land_idx.at[pl.ds(n * ROWS, ROWS)], land_idx_sem.at[n]
        )
        for n in range(8)
    ]
    for copy in land_copies:
        copy.start()

    lane = lax.broadcasted_iota(jnp.int32, (32, 128), 1)
    line = lax.broadcasted_iota(jnp.int32, (32, 128), 0)
    owner = order[...].reshape(1, 128)
    source = jnp.sum(
        jnp.where(owner == x_me * 32 + line, lane, 0), axis=1, keepdims=True
    )
    from_row = source // NCOL
    from_col = source - from_row * NCOL
    turn = (z_me - from_col + NCOL) % NZ
    dr = row - from_row
    dc = jnp.where(turn == 3, -1, turn)
    to_col = from_col + dc
    step = 2 * (dr + 1) + jnp.where(dc < 0, 1, 0)
    slot = jnp.where(
        dc == 0,
        jnp.where(dr == 0, 0, jnp.where(dr < 0, 3, 4)),
        1 + step + jnp.where(step >= 2, 2, 0),
    )
    good = (turn != 2) & (to_col >= 0) & (to_col < NCOL) & (dr >= -1) & (dr <= 1)
    place = jnp.where(good, (to_col // NZ) * 9 + slot, EMPTY)
    pick_vec[...] = jnp.broadcast_to(place, (32, 128))
    pick_copy = pltpu.make_async_copy(pick_vec, pick, pick_sem)
    pick_copy.start()

    lane8 = lax.broadcasted_iota(jnp.int32, (8, 128), 1)
    line8 = lax.broadcasted_iota(jnp.int32, (8, 128), 0)
    mine = jnp.sum(jnp.where(owner == col * 8 + line8, lane8, 0), axis=1, keepdims=True)
    at = lax.broadcasted_iota(jnp.int32, (8, WIDE), 1) // K
    here = at == lax.broadcasted_iota(jnp.int32, (8, WIDE), 0)
    mine = jnp.sum(jnp.where(here, jnp.broadcast_to(mine, (8, WIDE)), 0), axis=0, keepdims=True)
    mine_row = mine // NCOL
    mine_col = mine - mine_row * NCOL
    column = lax.broadcasted_iota(jnp.int32, (NCOL, WIDE), 0)
    near = (jnp.abs(mine_col - column) <= 1) & (jnp.abs(mine_row - row) <= 1)
    mask_out[...] = jnp.where(near, 1.0, 0.0)

    held[EMPTY] = jnp.zeros((HALF, 128), f32)
    for k in range(K + 1):
        zpad[k, 0:8, :] = jnp.zeros((8, 128), f32)
    zlines = zpad.reshape((K + 1) * PITCH, 128)

    eye = (
        lax.broadcasted_iota(jnp.int32, (128, 128), 0)
        == lax.broadcasted_iota(jnp.int32, (128, 128), 1)
    ).astype(bf16)

    def turn_chunk(i, carry):
        pltpu.make_async_copy(
            z_hbm.at[0, 0, :, pl.ds(i * PER, PER), :],
            zpad.at[pl.ds(0, K), pl.ds(8 + i * PER, PER), :],
            z_sem.at[i],
        ).wait()
        for u in range(PER):
            both = stacked(zlines[pl.ds(8 + i * PER + u, K, stride=PITCH), :])
            cells[pl.ds((i * PER + u) * 128, 128), 0 : 2 * K] = lax.dot_general(
                eye, both, (((1,), (1,)), ((), ())), preferred_element_type=f32
            )
        return carry

    lax.fori_loop(0, CHUNKS, turn_chunk, 0)

    for copy in send_copies:
        copy.wait()

    if remote:
        pl.semaphore_wait(barrier, 14)

    def near_copy(i, dr, dc):
        peer = (row + dr, col + dc)
        return pltpu.make_async_remote_copy(
            src_ref=sent.at[i],
            dst_ref=arrived.at[i],
            send_sem=near_send.at[i],
            recv_sem=near_recv.at[i],
            device_id=peer,
            device_id_type=MESH,
        )

    def inside(dr, dc):
        r, c = row + dr, col + dc
        return (r >= 0) & (r < NROW) & (c >= 0) & (c < NCOL)

    def send_step(t, odd, now, later):
        i = 2 * t + odd
        dr, dc, n = pair_step(t, odd)
        after = (i + 1) - (i + 1) // 8
        n_after = pair_step(after // 2, 1 - odd)[2]
        pltpu.make_async_copy(blocks_hbm.at[0, 0, n], blocks.at[i], block_sem.at[i]).wait()
        gather_rows(cells, send_idx, n_after * ROWS, later)
        keep = jnp.where(active[0, 0, n] == 1, 1.0, 0.0)
        times_block(now, blocks.at[i], keep, sent.at[i])
        if remote:
            @pl.when(inside(dr, dc))
            def _():
                near_copy(i, dr, dc).start()

    def send_two(t, carry):
        send_step(t, 0, rows_a, rows_b)
        send_step(t, 1, rows_b, rows_a)
        return carry

    gather_rows(cells, send_idx, pair_step(0, 0)[2] * ROWS, rows_a)
    lax.fori_loop(0, 4, send_two, 0)

    for copy in land_copies:
        copy.wait()

    first = lax.broadcasted_iota(jnp.int32, (K, 128), 1) == 0
    final = lax.broadcasted_iota(jnp.int32, (K, 128), 1) == 127

    def land_two(t, total):
        for odd, rows in ((0, rows_a), (1, rows_b)):
            gather_rows(cells, land_idx, pair_step(t, odd)[2] * ROWS, rows)
            landed[2 * t + odd] = flipped(rows)
        x0 = t * 32
        lines = [zlines[pl.ds(8 + x0 + u, K, stride=PITCH), :] for u in range(-1, 33)]
        for u in range(0, 32, 2):
            left, right = [], []
            for v in (u, u + 1):
                z = lines[v + 1]
                beside = lines[v] + lines[v + 2]
                beside += jnp.where(first, 0.0, pltpu.roll(z, 1, 1))
                beside += jnp.where(final, 0.0, pltpu.roll(z, 127, 1))
                image = (4.0 + coef[0, 0, pl.ds(x0 + v, 1), :]) * z - beside
                left.append(stacked(z))
                right.append(stacked(image))
            total = total + lax.dot_general(
                jnp.concatenate(left, axis=1),
                jnp.concatenate(right, axis=1),
                (((1,), (1,)), ((), ())),
                preferred_element_type=f32,
            )
        return total

    own = lax.fori_loop(0, 4, land_two, jnp.zeros((2 * K, 2 * K), f32))

    def put(slot, block):
        gap = jnp.zeros((HALF, 64 - K), f32)
        held[x_me * 9 + slot] = jnp.concatenate([block[:HALF], gap, block[HALF:], gap], axis=1)

    def x_copy(g, k):
        span = pl.ds(x_me * 9 + GROUPS[g][0], GROUPS[g][1])
        return pltpu.make_async_remote_copy(
            src_ref=held.at[span],
            dst_ref=held.at[span],
            send_sem=x_send.at[g * 3 + k - 1],
            recv_sem=x_recv.at[g * 3 + k - 1],
            device_id=(row, lax.rem(col + NZ * k, NCOL)),
            device_id_type=MESH,
        )

    put(0, unstack(own))
    for g, (slot, count, steps) in enumerate(GROUPS):
        slot = slot + count - 2
        for j, i in enumerate(steps):
            dr, dc = STEPS[i]
            if remote:
                @pl.when(inside(-dr, -dc))
                def _():
                    near_copy(i, dr, dc).wait_recv()
            there = stacked(arrived[i])
            put(slot + j, unstack(lax.dot_general(
                landed[i], there, (((1,), (1,)), ((), ())), preferred_element_type=f32
            )))
        if remote:
            for k in (2, 1, 3):
                x_copy(g, k).start()

    pick_copy.wait()
    if remote:
        for g in range(len(GROUPS)):
            for k in range(1, 4):
                x_copy(g, k).wait_recv()

    def z_copy(k):
        return pltpu.make_async_remote_copy(
            src_ref=strips.at[k],
            dst_ref=received.at[z_me],
            send_sem=z_send.at[k - 1],
            recv_sem=z_recv.at[k - 1],
            device_id=(row, x_me * NZ + lax.rem(z_me + k, NZ)),
            device_id_type=MESH,
        )

    for k in (2, 1, 3, 0):
        target = lax.rem(z_me + k, NZ)
        found = [held[pick[target * 8 + m, 0]] for m in range(8)]
        upper = jnp.concatenate([block[:, 0:K] for block in found], axis=1)
        lower = jnp.concatenate([block[:, 64 : 64 + K] for block in found], axis=1)
        strip = jnp.concatenate([upper, lower], axis=0)
        if k:
            strips[k] = strip
            if remote:
                z_copy(k).start()
        else:
            received[z_me] = strip

    if remote:
        for i, (dr, dc) in enumerate(STEPS):
            @pl.when(inside(dr, dc))
            def _():
                near_copy(i, dr, dc).wait_send()
        for g in range(len(GROUPS)):
            for k in range(1, 4):
                x_copy(g, k).wait_send()
        for k in range(1, 4):
            z_copy(k).wait_send()
        for k in range(1, 4):
            z_copy(k).wait_recv()
    strips_out[...] = received[...]


def place_strips(strips, mask, out):
    for p in range(NCOL):
        keep = mask[p : p + 1, :] > 0.5
        out[p * K : (p + 1) * K, :] = jnp.where(keep, strips[p % NZ], 0.0)


def assemble_call(remote, *args):
    vmem = pl.BlockSpec(memory_space=pltpu.VMEM)
    smem = pl.BlockSpec(memory_space=pltpu.SMEM)
    hbm = pl.BlockSpec(memory_space=pl.ANY)
    dma = pltpu.SemaphoreType.DMA
    return pl.pallas_call(
        functools.partial(assemble, remote),
        out_shape=(
            jax.ShapeDtypeStruct((NZ, K, WIDE), f32),
            jax.ShapeDtypeStruct((NCOL, WIDE), f32),
        ),
        in_specs=[hbm, vmem, hbm, hbm, hbm, smem, vmem],
        out_specs=(vmem, vmem),
        scratch_shapes=[
            pltpu.VMEM((K + 1, PITCH, 128), f32),
            pltpu.VMEM((CX * 128, 128), f32),
            pltpu.VMEM((8, ROWS, ROWS), f32),
            pltpu.VMEM((ROWS, 128), f32),
            pltpu.VMEM((ROWS, 128), f32),
            pltpu.VMEM((8, 2 * K, ROWS), bf16),
            pltpu.VMEM((8, K, ROWS), f32),
            pltpu.VMEM((8, K, ROWS), f32),
            pltpu.VMEM((EMPTY + 1, HALF, 128), f32),
            pltpu.VMEM((NZ, K, WIDE), f32),
            pltpu.VMEM((NZ, K, WIDE), f32),
            pltpu.VMEM((32, 128), jnp.int32),
            pltpu.SMEM((8 * ROWS,), jnp.int32),
            pltpu.SMEM((8 * ROWS,), jnp.int32),
            pltpu.SMEM((32, 128), jnp.int32),
            dma((CHUNKS,)), dma((8,)), dma((8,)), dma((8,)), dma,
            dma((8,)), dma((8,)), dma((12,)), dma((12,)), dma((3,)), dma((3,)),
        ],
        compiler_params=pltpu.CompilerParams(
            collective_id=0 if remote else None,
            has_side_effects=True,
            vmem_limit_bytes=56 * 2**20,
        ),
        cost_estimate=pl.CostEstimate(
            flops=2 * 10**9, bytes_accessed=18 * 10**6, transcendentals=0
        ),
    )(*args)


def on_device(zvecs, coef, blocks, send_idx, land_idx, active, order):
    strips, mask = assemble_call(True, zvecs, coef, blocks, send_idx, land_idx, active, order)
    return pl.pallas_call(
        place_strips,
        out_shape=jax.ShapeDtypeStruct((NCOL * K, WIDE), f32),
        in_specs=[pl.BlockSpec(memory_space=pltpu.VMEM)] * 2,
        out_specs=pl.BlockSpec(memory_space=pltpu.VMEM),
    )(strips, mask)


def solution(mesh):
    in_specs = (
        P("row", "col", None, None, None),
        P("row", "col", None, None),
        P("row", "col", None, None, None),
        P("row", "col", None, None),
        P("row", "col", None, None),
        P("row", "col", None),
        P(),
    )
    return jax.shard_map(
        on_device, mesh=mesh, in_specs=in_specs, out_specs=P("row", "col"), check_vma=False
    )
```

```python
import functools

import jax
import jax.numpy as jnp
from jax import lax
from jax.experimental import pallas as pl
from jax.experimental.pallas import tpu as pltpu
from jax.sharding import PartitionSpec as P

f32 = jnp.float32
bf16 = jnp.bfloat16
MESH = pl.DeviceIdType.MESH

K = 48
CX = 128
ROWS = 640
NROW = 8
NCOL = 16
NX = 4
NZ = 4
HALVES = 2
PER = CX // HALVES
TURN = 32
HALF = K // 2
WIDE = 8 * K
STEPS = ((-1, 1), (-1, -1), (0, 1), (0, -1), (-1, 0), (1, 0), (1, 1), (1, -1))
FINISH = (0, 2, 1, 3)
EMPTY = NX * 9


def split(x):
    high = x.astype(bf16)
    return high, (x - high.astype(f32)).astype(bf16)


def stacked(x):
    return jnp.concatenate(split(x), axis=0)


def unstack(product):
    return product[:K, :K] + product[K : 2 * K, :K] + product[:K, K : 2 * K]


def pair_step(t, odd):
    up = t // 2 - t // 3
    dr = (t - 1 - t // 3) * (1 - up) + up * (2 * odd - 1)
    dc = (1 - up) * (1 - 2 * odd)
    nine = (dr + 1) * 3 + dc + 1
    return dr, dc, nine - nine // 5


def gather_rows(cells, index, start, rows):
    for j in range(ROWS):
        rows[pl.ds(j, 1), :] = cells[pl.ds(index[start + j], 1), :]


def flipped(rows):
    return rows[...].astype(bf16).T[0 : 2 * K]


def times_block(rows, block, factor, out):
    picked = flipped(rows)
    for q0 in range(0, ROWS, 256):
        q1 = min(q0 + 256, ROWS)
        total, low_total = None, None
        for p0 in range(0, ROWS, 256):
            p1 = min(p0 + 256, ROWS)
            high, low = split(block[p0:p1, q0:q1])
            one = jnp.dot(picked[:, p0:p1], high, preferred_element_type=f32)
            two = jnp.dot(picked[0:K, p0:p1], low, preferred_element_type=f32)
            total = one if total is None else total + one
            low_total = two if low_total is None else low_total + two
        out[:, q0:q1] = (total[0:K] + total[K : 2 * K] + low_total) * factor


def assemble(
    remote,
    z_hbm, coef, blocks_hbm, send_hbm, land_hbm, active, order,
    out,
    zlines, zparts, cells, blocks, rows_a, rows_b, landed, sent, arrived, held, strips, received,
    pick_vec, send_idx, land_idx, pick,
    z_sem, block_sem, send_idx_sem, land_idx_sem, pick_sem,
    near_send, near_recv, x_send, x_recv, z_send, z_recv,
):
    row = lax.axis_index("row") if remote else 3
    col = lax.axis_index("col") if remote else 5
    x_me = col // NZ
    z_me = lax.rem(col, NZ)

    def lines_of(half):
        return zlines.at[pl.ds(half * PER, PER)]

    for half in range(HALVES):
        for k in range(K):
            pltpu.make_async_copy(
                z_hbm.at[0, 0, k, pl.ds(half * PER, PER), :],
                zlines.at[pl.ds(half * PER, PER), k, :],
                z_sem.at[half],
            ).start()
    send_copies = [
        pltpu.make_async_copy(
            send_hbm.at[0, 0, n], send_idx.at[pl.ds(n * ROWS, ROWS)], send_idx_sem.at[n]
        )
        for n in range(8)
    ]
    for copy in send_copies:
        copy.start()
    for i, (dr, dc) in enumerate(STEPS):
        nine = (dr + 1) * 3 + dc + 1
        pltpu.make_async_copy(
            blocks_hbm.at[0, 0, nine - nine // 5], blocks.at[i], block_sem.at[i]
        ).start()
    land_copies = [
        pltpu.make_async_copy(
            land_hbm.at[0, 0, n], land_idx.at[pl.ds(n * ROWS, ROWS)], land_idx_sem.at[n]
        )
        for n in range(8)
    ]
    for copy in land_copies:
        copy.start()

    if remote:
        barrier = pltpu.get_barrier_semaphore()
        for dr, dc in STEPS:
            peer = (lax.rem(row + dr + NROW, NROW), lax.rem(col + dc + NCOL, NCOL))
            pl.semaphore_signal(barrier, inc=1, device_id=peer, device_id_type=MESH)
        for k in range(1, 4):
            peer = (row, lax.rem(col + NZ * k, NCOL))
            pl.semaphore_signal(barrier, inc=1, device_id=peer, device_id_type=MESH)
            peer = (row, x_me * NZ + lax.rem(z_me + k, NZ))
            pl.semaphore_signal(barrier, inc=1, device_id=peer, device_id_type=MESH)

    zlines[CX] = jnp.zeros((K, 128), f32)
    eye = (
        lax.broadcasted_iota(jnp.int32, (128, 128), 0)
        == lax.broadcasted_iota(jnp.int32, (128, 128), 1)
    ).astype(bf16)

    def turn_chunk(i, carry):
        for u in range(TURN):
            both = stacked(zlines[i * TURN + u])
            zparts[i * TURN + u] = both
            cells[pl.ds((i * TURN + u) * 128, 128), 0 : 2 * K] = lax.dot_general(
                eye, both, (((1,), (1,)), ((), ())), preferred_element_type=f32
            )
        return carry

    for half in range(HALVES):
        pltpu.make_async_copy(lines_of(half), lines_of(half), z_sem.at[half]).wait()
        lax.fori_loop(half * PER // TURN, (half + 1) * PER // TURN, turn_chunk, 0)

    for copy in send_copies:
        copy.wait()

    if remote:
        pl.semaphore_wait(barrier, 14)

    def near_copy(i, dr, dc):
        peer = (row + dr, col + dc)
        return pltpu.make_async_remote_copy(
            src_ref=sent.at[i],
            dst_ref=arrived.at[i],
            send_sem=near_send.at[i],
            recv_sem=near_recv.at[i],
            device_id=peer,
            device_id_type=MESH,
        )

    def inside(dr, dc):
        r, c = row + dr, col + dc
        return (r >= 0) & (r < NROW) & (c >= 0) & (c < NCOL)

    def send_step(t, odd, now, later):
        i = 2 * t + odd
        dr, dc, n = pair_step(t, odd)
        after = (i + 1) - (i + 1) // 8
        n_after = pair_step(after // 2, 1 - odd)[2]
        pltpu.make_async_copy(blocks_hbm.at[0, 0, n], blocks.at[i], block_sem.at[i]).wait()
        gather_rows(cells, send_idx, n_after * ROWS, later)
        keep = jnp.where(active[0, 0, n] == 1, 1.0, 0.0)
        times_block(now, blocks.at[i], keep, sent.at[i])
        if remote:
            @pl.when(inside(dr, dc))
            def _():
                near_copy(i, dr, dc).start()

    def send_two(t, carry):
        send_step(t, 0, rows_a, rows_b)
        send_step(t, 1, rows_b, rows_a)
        return carry

    gather_rows(cells, send_idx, pair_step(0, 0)[2] * ROWS, rows_a)
    lax.fori_loop(0, 4, send_two, 0)

    lane = lax.broadcasted_iota(jnp.int32, (32, 128), 1)
    line = lax.broadcasted_iota(jnp.int32, (32, 128), 0)
    owner = order[...].reshape(1, 128)
    source = jnp.sum(
        jnp.where(owner == x_me * 32 + line, lane, 0), axis=1, keepdims=True
    )
    from_row = source // NCOL
    from_col = source - from_row * NCOL
    turn = (z_me - from_col + NCOL) % NZ
    dr = row - from_row
    dc = jnp.where(turn == 3, -1, turn)
    to_col = from_col + dc
    step = 2 * (dr + 1) + jnp.where(dc < 0, 1, 0)
    slot = jnp.where(
        dc == 0,
        jnp.where(dr == 0, 0, jnp.where(dr < 0, 5, 6)),
        1 + step + jnp.where(dr > 0, 2, 0),
    )
    good = (turn != 2) & (to_col >= 0) & (to_col < NCOL) & (dr >= -1) & (dr <= 1)
    place = jnp.where(good, (to_col // NZ) * 9 + slot, EMPTY)
    pick_vec[...] = jnp.broadcast_to(place, (32, 128))
    pick_copy = pltpu.make_async_copy(pick_vec, pick, pick_sem)
    pick_copy.start()

    lane8 = lax.broadcasted_iota(jnp.int32, (8, 128), 1)
    line8 = lax.broadcasted_iota(jnp.int32, (8, 128), 0)
    mine = jnp.sum(jnp.where(owner == col * 8 + line8, lane8, 0), axis=1, keepdims=True)
    at = lax.broadcasted_iota(jnp.int32, (8, WIDE), 1) // K
    here = at == lax.broadcasted_iota(jnp.int32, (8, WIDE), 0)
    mine = jnp.sum(jnp.where(here, jnp.broadcast_to(mine, (8, WIDE)), 0), axis=0, keepdims=True)
    mine_row = mine // NCOL
    mine_col = mine - mine_row * NCOL
    column = lax.broadcasted_iota(jnp.int32, (NCOL, WIDE), 0)
    near = (jnp.abs(mine_col - column) <= 1) & (jnp.abs(mine_row - row) <= 1)

    held[EMPTY] = jnp.zeros((HALF, 128), f32)

    for copy in land_copies:
        copy.wait()

    final = lax.broadcasted_iota(jnp.int32, (K, 128), 1) == 127

    def land_two(t, total):
        for odd in (0, 1):
            gather_rows(cells, land_idx, pair_step(t, odd)[2] * ROWS, landed.at[2 * t + odd])
        x0 = t * 32
        left, right = [], []
        for v in range(32):
            z = zlines[x0 + v]
            beside = zlines[x0 + v + 1] + jnp.where(final, 0.0, pltpu.roll(z, 127, 1))
            half_image = (2.0 + 0.5 * coef[0, 0, pl.ds(x0 + v, 1), :]) * z - beside
            left.append(zparts[x0 + v])
            right.append(stacked(half_image))
        return total + lax.dot_general(
            jnp.concatenate(left, axis=1),
            jnp.concatenate(right, axis=1),
            (((1,), (1,)), ((), ())),
            preferred_element_type=f32,
        )

    own = unstack(lax.fori_loop(0, 4, land_two, jnp.zeros((2 * K, 2 * K), f32)))
    own = own + own.T

    def put(slot, block):
        gap = jnp.zeros((HALF, 64 - K), f32)
        held[x_me * 9 + slot] = jnp.concatenate([block[:HALF], gap, block[HALF:], gap], axis=1)

    def x_copy(t, k):
        span = pl.ds(x_me * 9 + (2 * t + 1 if t else 0), 2 if t else 3)
        return pltpu.make_async_remote_copy(
            src_ref=held.at[span],
            dst_ref=held.at[span],
            send_sem=x_send.at[t * 3 + k - 1],
            recv_sem=x_recv.at[t * 3 + k - 1],
            device_id=(row, lax.rem(col + NZ * k, NCOL)),
            device_id_type=MESH,
        )

    put(0, own)
    for t in FINISH:
        for i in (2 * t, 2 * t + 1):
            dr, dc = STEPS[i]
            if remote:
                @pl.when(inside(-dr, -dc))
                def _():
                    near_copy(i, dr, dc).wait_recv()
            product = jnp.dot(
                stacked(arrived[i]), landed[i].astype(bf16), preferred_element_type=f32
            )
            put(i + 1, unstack(product.T))
        if remote:
            for k in (2, 1, 3):
                x_copy(t, k).start()

    pick_copy.wait()
    if remote:
        for g in range(4):
            for k in range(1, 4):
                x_copy(g, k).wait_recv()

    def z_copy(k):
        return pltpu.make_async_remote_copy(
            src_ref=strips.at[k],
            dst_ref=received.at[z_me],
            send_sem=z_send.at[k - 1],
            recv_sem=z_recv.at[k - 1],
            device_id=(row, x_me * NZ + lax.rem(z_me + k, NZ)),
            device_id_type=MESH,
        )

    for k in (2, 1, 3, 0):
        target = lax.rem(z_me + k, NZ)
        found = [held[pick[target * 8 + m, 0]] for m in range(8)]
        upper = jnp.concatenate([block[:, 0:K] for block in found], axis=1)
        lower = jnp.concatenate([block[:, 64 : 64 + K] for block in found], axis=1)
        strip = jnp.concatenate([upper, lower], axis=0)
        if k:
            strips[k] = strip
            if remote:
                z_copy(k).start()
        else:
            received[z_me] = strip

    if remote:
        for i, (dr, dc) in enumerate(STEPS):
            @pl.when(inside(dr, dc))
            def _():
                near_copy(i, dr, dc).wait_send()
        for g in range(4):
            for k in range(1, 4):
                x_copy(g, k).wait_send()
        for k in range(1, 4):
            z_copy(k).wait_send()
        for k in range(1, 4):
            z_copy(k).wait_recv()
    for p in range(NCOL):
        out[p * K : (p + 1) * K, :] = jnp.where(near[p : p + 1, :], received[p % NZ], 0.0)


def assemble_call(remote, *args):
    vmem = pl.BlockSpec(memory_space=pltpu.VMEM)
    smem = pl.BlockSpec(memory_space=pltpu.SMEM)
    hbm = pl.BlockSpec(memory_space=pl.ANY)
    dma = pltpu.SemaphoreType.DMA
    return pl.pallas_call(
        functools.partial(assemble, remote),
        out_shape=jax.ShapeDtypeStruct((NCOL * K, WIDE), f32),
        in_specs=[hbm, vmem, hbm, hbm, hbm, smem, vmem],
        out_specs=vmem,
        scratch_shapes=[
            pltpu.VMEM((CX + 1, K, 128), f32),
            pltpu.VMEM((CX, 2 * K, 128), bf16),
            pltpu.VMEM((CX * 128, 128), f32),
            pltpu.VMEM((8, ROWS, ROWS), f32),
            pltpu.VMEM((ROWS, 128), f32),
            pltpu.VMEM((ROWS, 128), f32),
            pltpu.VMEM((8, ROWS, 128), f32),
            pltpu.VMEM((8, K, ROWS), f32),
            pltpu.VMEM((8, K, ROWS), f32),
            pltpu.VMEM((EMPTY + 1, HALF, 128), f32),
            pltpu.VMEM((NZ, K, WIDE), f32),
            pltpu.VMEM((NZ, K, WIDE), f32),
            pltpu.VMEM((32, 128), jnp.int32),
            pltpu.SMEM((8 * ROWS,), jnp.int32),
            pltpu.SMEM((8 * ROWS,), jnp.int32),
            pltpu.SMEM((32, 128), jnp.int32),
            dma((HALVES,)), dma((8,)), dma((8,)), dma((8,)), dma,
            dma((8,)), dma((8,)), dma((12,)), dma((12,)), dma((3,)), dma((3,)),
        ],
        compiler_params=pltpu.CompilerParams(
            collective_id=0 if remote else None,
            has_side_effects=True,
            vmem_limit_bytes=56 * 2**20,
        ),
        cost_estimate=pl.CostEstimate(
            flops=2 * 10**9, bytes_accessed=18 * 10**6, transcendentals=0
        ),
    )(*args)


def on_device(zvecs, coef, blocks, send_idx, land_idx, active, order):
    return assemble_call(True, zvecs, coef, blocks, send_idx, land_idx, active, order)


def solution(mesh):
    in_specs = (
        P("row", "col", None, None, None),
        P("row", "col", None, None),
        P("row", "col", None, None, None),
        P("row", "col", None, None),
        P("row", "col", None, None),
        P("row", "col", None),
        P(),
    )
    return jax.shard_map(
        on_device, mesh=mesh, in_specs=in_specs, out_specs=P("row", "col"), check_vma=False
    )
```

```python
import functools

import jax
import jax.numpy as jnp
from jax import lax
from jax.experimental import pallas as pl
from jax.experimental.pallas import tpu as pltpu
from jax.sharding import PartitionSpec as P

f32 = jnp.float32
bf16 = jnp.bfloat16
MESH = pl.DeviceIdType.MESH

K = 48
CX = 128
ROWS = 640
NROW = 8
NCOL = 16
NX = 4
NZ = 4
HALVES = 2
PER = CX // HALVES
TURN = 32
HALF = K // 2
WIDE = 8 * K
STEPS = ((-1, 1), (-1, -1), (0, 1), (0, -1), (-1, 0), (1, 0), (1, 1), (1, -1))
GROUPS = ((0, 2), (2, 2), (4, 3), (7, 2))
SLOTS = (0, 1, 5, 6, 2, 3, 7, 8)
OWN_SLOT = 4
EMPTY = NX * 9


def split(x):
    high = x.astype(bf16)
    return high, (x - high.astype(f32)).astype(bf16)


def stacked(x):
    return jnp.concatenate(split(x), axis=0)


def unstack(product):
    return product[:K, :K] + product[K : 2 * K, :K] + product[:K, K : 2 * K]


def direction(i):
    nine = (STEPS[i][0] + 1) * 3 + STEPS[i][1] + 1
    return nine - nine // 5


def gather_rows(cells, index, n, rows):
    for j in range(ROWS):
        rows[pl.ds(j, 1), :] = cells[pl.ds(index[n, j], 1), :]


def times_block(picked, block, factor, out):
    for q0 in range(0, ROWS, 256):
        q1 = min(q0 + 256, ROWS)
        total, low_total = None, None
        for p0 in range(0, ROWS, 256):
            p1 = min(p0 + 256, ROWS)
            high, low = split(block[p0:p1, q0:q1])
            one = jnp.dot(picked[:, p0:p1], high, preferred_element_type=f32)
            two = jnp.dot(picked[0:K, p0:p1], low, preferred_element_type=f32)
            total = one if total is None else total + one
            low_total = two if low_total is None else low_total + two
        out[:, q0:q1] = (total[0:K] + total[K : 2 * K] + low_total) * factor


def assemble(
    remote,
    z_hbm, coef, blocks_hbm, send_hbm, land_hbm, active, order,
    strips_out, mask_out,
    zlines, zparts, cells, blocks, rows_a, rows_b, picked_a, picked_b, landed, sent, arrived,
    held, strips, received,
    pick_vec, send_idx, land_idx, pick,
    z_sem, block_sem, send_idx_sem, land_idx_sem, pick_sem,
    near_send, near_recv, x_send, x_recv, z_send, z_recv,
):
    row = lax.axis_index("row") if remote else 3
    col = lax.axis_index("col") if remote else 5
    x_me = col // NZ
    z_me = lax.rem(col, NZ)

    def lines_of(half):
        return zlines.at[pl.ds(half * PER, PER)]

    for half in range(HALVES):
        for k in range(K):
            pltpu.make_async_copy(
                z_hbm.at[0, 0, k, pl.ds(half * PER, PER), :],
                zlines.at[pl.ds(half * PER, PER), k, :],
                z_sem.at[half],
            ).start()
    send_copy = pltpu.make_async_copy(send_hbm.at[0, 0], send_idx, send_idx_sem)
    send_copy.start()
    block_copies = [
        pltpu.make_async_copy(blocks_hbm.at[0, 0, direction(i)], blocks.at[i], block_sem.at[i])
        for i in range(8)
    ]
    for copy in block_copies:
        copy.start()
    land_copy = pltpu.make_async_copy(land_hbm.at[0, 0], land_idx, land_idx_sem)
    land_copy.start()

    if remote:
        barrier = pltpu.get_barrier_semaphore()
        for dr, dc in STEPS:
            peer = (lax.rem(row + dr + NROW, NROW), lax.rem(col + dc + NCOL, NCOL))
            pl.semaphore_signal(barrier, inc=1, device_id=peer, device_id_type=MESH)
        for k in range(1, 4):
            peer = (row, lax.rem(col + NZ * k, NCOL))
            pl.semaphore_signal(barrier, inc=1, device_id=peer, device_id_type=MESH)
            peer = (row, x_me * NZ + lax.rem(z_me + k, NZ))
            pl.semaphore_signal(barrier, inc=1, device_id=peer, device_id_type=MESH)

    zlines[CX] = jnp.zeros((K, 128), f32)
    def turn_chunk(i, carry):
        for u in range(TURN):
            both = stacked(zlines[i * TURN + u])
            zparts[i * TURN + u] = both
            cells[pl.ds((i * TURN + u) * 128, 128), 0 : 2 * K] = both.T.astype(f32)
        return carry

    for half in range(HALVES):
        pltpu.make_async_copy(lines_of(half), lines_of(half), z_sem.at[half]).wait()
        lax.fori_loop(half * PER // TURN, (half + 1) * PER // TURN, turn_chunk, 0)

    send_copy.wait()

    if remote:
        pl.semaphore_wait(barrier, 14)

    def near_copy(i, dr, dc):
        peer = (row + dr, col + dc)
        return pltpu.make_async_remote_copy(
            src_ref=sent.at[i],
            dst_ref=arrived.at[i],
            send_sem=near_send.at[i],
            recv_sem=near_recv.at[i],
            device_id=peer,
            device_id_type=MESH,
        )

    def inside(dr, dc):
        r, c = row + dr, col + dc
        return (r >= 0) & (r < NROW) & (c >= 0) & (c < NCOL)

    rows = (rows_a, rows_b)
    picked = (picked_a, picked_b)

    def pick_up(i):
        gather_rows(cells, send_idx, direction(i), rows[i % 2])

    def flip(i):
        picked[i % 2][...] = rows[i % 2][...].astype(bf16).T[0 : 2 * K]

    def multiply(i):
        block_copies[i].wait()
        keep = jnp.where(active[0, 0, direction(i)] == 1, 1.0, 0.0)
        times_block(picked[i % 2], blocks.at[i], keep, sent.at[i])
        if remote:
            dr, dc = STEPS[i]

            @pl.when(inside(dr, dc))
            def _():
                near_copy(i, dr, dc).start()

    pick_up(0)
    flip(0)
    multiply(0)
    pick_up(1)
    flip(1)
    for i in range(1, 8):
        if i < 7:
            pick_up(i + 1)
        multiply(i)
        if i < 7:
            flip(i + 1)

    lane = lax.broadcasted_iota(jnp.int32, (32, 128), 1)
    line = lax.broadcasted_iota(jnp.int32, (32, 128), 0)
    owner = order[...].reshape(1, 128)
    source = jnp.sum(
        jnp.where(owner == x_me * 32 + line, lane, 0), axis=1, keepdims=True
    )
    from_row = source // NCOL
    from_col = source - from_row * NCOL
    turn = (z_me - from_col + NCOL) % NZ
    dr = row - from_row
    dc = jnp.where(turn == 3, -1, turn)
    to_col = from_col + dc
    step = 2 * (dr + 1) + jnp.where(dc < 0, 1, 0)
    slot = jnp.where(
        dc == 0,
        jnp.where(dr == 0, OWN_SLOT, jnp.where(dr < 0, 2, 3)),
        step + jnp.where(step >= 2, 3, 0),
    )
    good = (turn != 2) & (to_col >= 0) & (to_col < NCOL) & (dr >= -1) & (dr <= 1)
    place = jnp.where(good, (to_col // NZ) * 9 + slot, EMPTY)
    pick_vec[...] = jnp.broadcast_to(place, (32, 128))
    pick_copy = pltpu.make_async_copy(pick_vec, pick, pick_sem)
    pick_copy.start()

    lane8 = lax.broadcasted_iota(jnp.int32, (8, 128), 1)
    line8 = lax.broadcasted_iota(jnp.int32, (8, 128), 0)
    mine = jnp.sum(jnp.where(owner == col * 8 + line8, lane8, 0), axis=1, keepdims=True)
    at = lax.broadcasted_iota(jnp.int32, (8, WIDE), 1) // K
    here = at == lax.broadcasted_iota(jnp.int32, (8, WIDE), 0)
    mine = jnp.sum(jnp.where(here, jnp.broadcast_to(mine, (8, WIDE)), 0), axis=0, keepdims=True)
    mine_row = mine // NCOL
    mine_col = mine - mine_row * NCOL
    column = lax.broadcasted_iota(jnp.int32, (NCOL, WIDE), 0)
    near = (jnp.abs(mine_col - column) <= 1) & (jnp.abs(mine_row - row) <= 1)

    mask_out[...] = jnp.where(near, 1.0, 0.0)
    held[EMPTY] = jnp.zeros((HALF, 128), f32)

    land_copy.wait()
    final = lax.broadcasted_iota(jnp.int32, (K, 128), 1) == 127

    def land(t):
        for i in (2 * t, 2 * t + 1):
            gather_rows(cells, land_idx, direction(i), landed.at[i])

    def gram(x0):
        left, right = [], []
        for x in range(x0, x0 + CX // 4):
            z = zlines[x]
            beside = zlines[x + 1] + jnp.where(final, 0.0, pltpu.roll(z, 127, 1))
            half_image = (2.0 + 0.5 * coef[0, 0, x : x + 1, :]) * z - beside
            left.append(zparts[x])
            right.append(stacked(half_image))
        return lax.dot_general(
            jnp.concatenate(left, axis=1),
            jnp.concatenate(right, axis=1),
            (((1,), (1,)), ((), ())),
            preferred_element_type=f32,
        )

    def put(slot, block):
        gap = jnp.zeros((HALF, 64 - K), f32)
        held[x_me * 9 + slot] = jnp.concatenate([block[:HALF], gap, block[HALF:], gap], axis=1)

    def x_copy(g, k):
        span = pl.ds(x_me * 9 + GROUPS[g][0], GROUPS[g][1])
        return pltpu.make_async_remote_copy(
            src_ref=held.at[span],
            dst_ref=held.at[span],
            send_sem=x_send.at[g * 3 + k - 1],
            recv_sem=x_recv.at[g * 3 + k - 1],
            device_id=(row, lax.rem(col + NZ * k, NCOL)),
            device_id_type=MESH,
        )

    def pair(t):
        for i in (2 * t, 2 * t + 1):
            dr, dc = STEPS[i]
            if remote:
                @pl.when(inside(-dr, -dc))
                def _():
                    near_copy(i, dr, dc).wait_recv()
            product = jnp.dot(
                stacked(arrived[i]), landed[i].astype(bf16), preferred_element_type=f32
            )
            put(SLOTS[i], unstack(product.T))

    def send_along_x(g):
        if remote:
            for k in (2, 1, 3):
                x_copy(g, k).start()

    land(0)
    own = gram(0)
    land(2)
    own += gram(CX // 4)
    pair(0)
    send_along_x(0)
    land(1)
    own += gram(CX // 2)
    pair(2)
    send_along_x(1)
    land(3)
    own += gram(3 * CX // 4)
    own = unstack(own)
    put(OWN_SLOT, own + own.T)
    pair(1)
    send_along_x(2)
    pair(3)
    send_along_x(3)

    pick_copy.wait()
    if remote:
        for g in range(4):
            for k in range(1, 4):
                x_copy(g, k).wait_recv()

    def z_copy(k):
        return pltpu.make_async_remote_copy(
            src_ref=strips.at[k],
            dst_ref=received.at[z_me],
            send_sem=z_send.at[k - 1],
            recv_sem=z_recv.at[k - 1],
            device_id=(row, x_me * NZ + lax.rem(z_me + k, NZ)),
            device_id_type=MESH,
        )

    for k in (2, 1, 3, 0):
        target = lax.rem(z_me + k, NZ)
        found = [held[pick[target * 8 + m, 0]] for m in range(8)]
        upper = jnp.concatenate([block[:, 0:K] for block in found], axis=1)
        lower = jnp.concatenate([block[:, 64 : 64 + K] for block in found], axis=1)
        strip = jnp.concatenate([upper, lower], axis=0)
        if k:
            strips[k] = strip
            if remote:
                z_copy(k).start()
        else:
            received[z_me] = strip

    if remote:
        for i, (dr, dc) in enumerate(STEPS):
            @pl.when(inside(dr, dc))
            def _():
                near_copy(i, dr, dc).wait_send()
        for g in range(4):
            for k in range(1, 4):
                x_copy(g, k).wait_send()
        for k in range(1, 4):
            z_copy(k).wait_send()
        for k in range(1, 4):
            z_copy(k).wait_recv()
    strips_out[...] = received[...]


def place_strips(strips, mask, out):
    for p in range(NCOL):
        keep = mask[p : p + 1, :] > 0.5
        out[p * K : (p + 1) * K, :] = jnp.where(keep, strips[p % NZ], 0.0)


def assemble_call(remote, *args):
    vmem = pl.BlockSpec(memory_space=pltpu.VMEM)
    smem = pl.BlockSpec(memory_space=pltpu.SMEM)
    hbm = pl.BlockSpec(memory_space=pl.ANY)
    dma = pltpu.SemaphoreType.DMA
    return pl.pallas_call(
        functools.partial(assemble, remote),
        out_shape=(
            jax.ShapeDtypeStruct((NZ, K, WIDE), f32),
            jax.ShapeDtypeStruct((NCOL, WIDE), f32),
        ),
        in_specs=[hbm, vmem, hbm, hbm, hbm, smem, vmem],
        out_specs=(vmem, vmem),
        scratch_shapes=[
            pltpu.VMEM((CX + 1, K, 128), f32),
            pltpu.VMEM((CX, 2 * K, 128), bf16),
            pltpu.VMEM((CX * 128, 128), f32),
            pltpu.VMEM((8, ROWS, ROWS), f32),
            pltpu.VMEM((ROWS, 128), f32),
            pltpu.VMEM((ROWS, 128), f32),
            pltpu.VMEM((2 * K, ROWS), bf16),
            pltpu.VMEM((2 * K, ROWS), bf16),
            pltpu.VMEM((8, ROWS, 128), f32),
            pltpu.VMEM((8, K, ROWS), f32),
            pltpu.VMEM((8, K, ROWS), f32),
            pltpu.VMEM((EMPTY + 1, HALF, 128), f32),
            pltpu.VMEM((NZ, K, WIDE), f32),
            pltpu.VMEM((NZ, K, WIDE), f32),
            pltpu.VMEM((32, 128), jnp.int32),
            pltpu.SMEM((8, ROWS), jnp.int32),
            pltpu.SMEM((8, ROWS), jnp.int32),
            pltpu.SMEM((32, 128), jnp.int32),
            dma((HALVES,)), dma((8,)), dma, dma, dma,
            dma((8,)), dma((8,)), dma((12,)), dma((12,)), dma((3,)), dma((3,)),
        ],
        compiler_params=pltpu.CompilerParams(
            collective_id=0 if remote else None,
            has_side_effects=True,
            vmem_limit_bytes=56 * 2**20,
        ),
        cost_estimate=pl.CostEstimate(
            flops=2 * 10**9, bytes_accessed=18 * 10**6, transcendentals=0
        ),
    )(*args)


def on_device(zvecs, coef, blocks, send_idx, land_idx, active, order):
    strips, mask = assemble_call(True, zvecs, coef, blocks, send_idx, land_idx, active, order)
    return pl.pallas_call(
        place_strips,
        out_shape=jax.ShapeDtypeStruct((NCOL * K, WIDE), f32),
        in_specs=[pl.BlockSpec(memory_space=pltpu.VMEM)] * 2,
        out_specs=pl.BlockSpec(memory_space=pltpu.VMEM),
    )(strips, mask)


def solution(mesh):
    in_specs = (
        P("row", "col", None, None, None),
        P("row", "col", None, None),
        P("row", "col", None, None, None),
        P("row", "col", None, None),
        P("row", "col", None, None),
        P("row", "col", None),
        P(),
    )
    return jax.shard_map(
        on_device, mesh=mesh, in_specs=in_specs, out_specs=P("row", "col"), check_vma=False
    )
```

```python
import functools

import jax
import jax.numpy as jnp
from jax import lax
from jax.experimental import pallas as pl
from jax.experimental.pallas import tpu as pltpu
from jax.sharding import PartitionSpec as P

f32 = jnp.float32
bf16 = jnp.bfloat16
MESH = pl.DeviceIdType.MESH

K = 48
CX = 128
ROWS = 640
NROW = 8
NCOL = 16
NX = 4
NZ = 4
HALVES = 2
PER = CX // HALVES
TURN = 32
HALF = K // 2
WIDE = 8 * K
STEPS = ((-1, 1), (-1, -1), (0, 1), (0, -1), (-1, 0), (1, 0), (1, 1), (1, -1))
GROUPS = ((0, 2), (2, 2), (4, 3), (7, 2))
SLOTS = (0, 1, 5, 6, 2, 3, 7, 8)
OWN_SLOT = 4
EMPTY = NX * 9


def split(x):
    high = x.astype(bf16)
    return high, (x - high.astype(f32)).astype(bf16)


def stacked(x):
    return jnp.concatenate(split(x), axis=0)


def unstack(product):
    return product[:K, :K] + product[K : 2 * K, :K] + product[:K, K : 2 * K]


def direction(i):
    nine = (STEPS[i][0] + 1) * 3 + STEPS[i][1] + 1
    return nine - nine // 5


def gathering(cells, index, n, rows, batch):
    for j in range(ROWS):
        rows[pl.ds(j, 1), :] = cells[pl.ds(index[n, j], 1), :]
        if j % batch == batch - 1:
            yield


def finish(steps):
    for _ in steps:
        pass


def times_block(picked, block, factor, out, beside):
    for q0 in range(0, ROWS, 256):
        q1 = min(q0 + 256, ROWS)
        total, low_total = None, None
        for p0 in range(0, ROWS, 256):
            p1 = min(p0 + 256, ROWS)
            high, low = split(block[p0:p1, q0:q1])
            one = jnp.dot(picked[:, p0:p1], high, preferred_element_type=f32)
            two = jnp.dot(picked[0:K, p0:p1], low, preferred_element_type=f32)
            total = one if total is None else total + one
            low_total = two if low_total is None else low_total + two
            next(beside, None)
        out[:, q0:q1] = (total[0:K] + total[K : 2 * K] + low_total) * factor
    finish(beside)


def assemble(
    remote,
    z_hbm, coef_hbm, blocks_hbm, send_hbm, land_hbm, active_hbm, order_hbm,
    strips_out, mask_out,
    zlines, zparts, cells, blocks, rows_a, rows_b, picked_a, picked_b, landed, sent, arrived,
    held, strips, received, coef, order,
    pick_vec, send_idx, land_idx, active, pick,
    z_sem, block_sem, send_idx_sem, land_idx_sem, small_sem, pick_sem,
    near_send, near_recv, x_send, x_recv, z_send, z_recv,
):
    row = lax.axis_index("row") if remote else 3
    col = lax.axis_index("col") if remote else 5
    x_me = col // NZ
    z_me = lax.rem(col, NZ)

    def lines_of(half):
        return zlines.at[pl.ds(half * PER, PER)]

    send_copy = pltpu.make_async_copy(send_hbm.at[0, 0], send_idx, send_idx_sem)
    send_copy.start()
    for half in range(HALVES):
        for k in range(K):
            pltpu.make_async_copy(
                z_hbm.at[0, 0, k, pl.ds(half * PER, PER), :],
                zlines.at[pl.ds(half * PER, PER), k, :],
                z_sem.at[half],
            ).start()
    active_copy = pltpu.make_async_copy(active_hbm.at[0], active, small_sem.at[0])
    active_copy.start()
    coef_copy = pltpu.make_async_copy(coef_hbm.at[0, 0], coef, small_sem.at[1])
    order_copy = pltpu.make_async_copy(order_hbm, order, small_sem.at[2])
    land_copy = pltpu.make_async_copy(land_hbm.at[0, 0], land_idx, land_idx_sem)
    block_copies = [
        pltpu.make_async_copy(blocks_hbm.at[0, 0, direction(i)], blocks.at[i], block_sem.at[i])
        for i in range(8)
    ]

    if remote:
        barrier = pltpu.get_barrier_semaphore()
        for dr, dc in STEPS:
            peer = (lax.rem(row + dr + NROW, NROW), lax.rem(col + dc + NCOL, NCOL))
            pl.semaphore_signal(barrier, inc=1, device_id=peer, device_id_type=MESH)
        for k in range(1, 4):
            peer = (row, lax.rem(col + NZ * k, NCOL))
            pl.semaphore_signal(barrier, inc=1, device_id=peer, device_id_type=MESH)
            peer = (row, x_me * NZ + lax.rem(z_me + k, NZ))
            pl.semaphore_signal(barrier, inc=1, device_id=peer, device_id_type=MESH)

    zlines[CX] = jnp.zeros((K, 128), f32)
    def turn_chunk(i, carry):
        for u in range(TURN):
            both = stacked(zlines[i * TURN + u])
            zparts[i * TURN + u] = both
            cells[pl.ds((i * TURN + u) * 128, 128), 0 : 2 * K] = both.T.astype(f32)
        return carry

    for half in range(HALVES):
        pltpu.make_async_copy(lines_of(half), lines_of(half), z_sem.at[half]).wait()
        if half == HALVES - 1:
            for copy in block_copies + [order_copy, coef_copy, land_copy]:
                copy.start()
        lax.fori_loop(half * PER // TURN, (half + 1) * PER // TURN, turn_chunk, 0)

    send_copy.wait()
    active_copy.wait()

    if remote:
        pl.semaphore_wait(barrier, 14)

    def near_copy(i, dr, dc):
        peer = (row + dr, col + dc)
        return pltpu.make_async_remote_copy(
            src_ref=sent.at[i],
            dst_ref=arrived.at[i],
            send_sem=near_send.at[i],
            recv_sem=near_recv.at[i],
            device_id=peer,
            device_id_type=MESH,
        )

    def inside(dr, dc):
        r, c = row + dr, col + dc
        return (r >= 0) & (r < NROW) & (c >= 0) & (c < NCOL)

    rows = (rows_a, rows_b)
    picked = (picked_a, picked_b)

    def pick_up(i):
        return gathering(cells, send_idx, direction(i), rows[i % 2], 72)

    def flip(i):
        picked[i % 2][...] = rows[i % 2][...].astype(bf16).T[0 : 2 * K]

    def multiply(i, beside=iter(())):
        block_copies[i].wait()
        keep = jnp.where(active[0, direction(i)] == 1, 1.0, 0.0)
        times_block(picked[i % 2], blocks.at[i], keep, sent.at[i], beside)
        if remote:
            dr, dc = STEPS[i]

            @pl.when(inside(dr, dc))
            def _():
                near_copy(i, dr, dc).start()

    finish(pick_up(0))
    flip(0)
    multiply(0)
    finish(pick_up(1))
    flip(1)
    for i in range(1, 7):
        multiply(i, pick_up(i + 1))
        flip(i + 1)
    multiply(7)

    order_copy.wait()
    lane = lax.broadcasted_iota(jnp.int32, (32, 128), 1)
    line = lax.broadcasted_iota(jnp.int32, (32, 128), 0)
    owner = order[...].reshape(1, 128)
    source = jnp.sum(
        jnp.where(owner == x_me * 32 + line, lane, 0), axis=1, keepdims=True
    )
    from_row = source // NCOL
    from_col = source - from_row * NCOL
    turn = (z_me - from_col + NCOL) % NZ
    dr = row - from_row
    dc = jnp.where(turn == 3, -1, turn)
    to_col = from_col + dc
    step = 2 * (dr + 1) + jnp.where(dc < 0, 1, 0)
    slot = jnp.where(
        dc == 0,
        jnp.where(dr == 0, OWN_SLOT, jnp.where(dr < 0, 2, 3)),
        step + jnp.where(step >= 2, 3, 0),
    )
    good = (turn != 2) & (to_col >= 0) & (to_col < NCOL) & (dr >= -1) & (dr <= 1)
    place = jnp.where(good, (to_col // NZ) * 9 + slot, EMPTY)
    pick_vec[...] = jnp.broadcast_to(place, (32, 128))
    pick_copy = pltpu.make_async_copy(pick_vec, pick, pick_sem)
    pick_copy.start()

    lane8 = lax.broadcasted_iota(jnp.int32, (8, 128), 1)
    line8 = lax.broadcasted_iota(jnp.int32, (8, 128), 0)
    mine = jnp.sum(jnp.where(owner == col * 8 + line8, lane8, 0), axis=1, keepdims=True)
    at = lax.broadcasted_iota(jnp.int32, (8, WIDE), 1) // K
    here = at == lax.broadcasted_iota(jnp.int32, (8, WIDE), 0)
    mine = jnp.sum(jnp.where(here, jnp.broadcast_to(mine, (8, WIDE)), 0), axis=0, keepdims=True)
    mine_row = mine // NCOL
    mine_col = mine - mine_row * NCOL
    column = lax.broadcasted_iota(jnp.int32, (NCOL, WIDE), 0)
    near = (jnp.abs(mine_col - column) <= 1) & (jnp.abs(mine_row - row) <= 1)

    mask_out[...] = jnp.where(near, 1.0, 0.0)
    held[EMPTY] = jnp.zeros((HALF, 128), f32)

    land_copy.wait()
    coef_copy.wait()
    final = lax.broadcasted_iota(jnp.int32, (K, 128), 1) == 127

    def land(t, x0, total):
        beside = (
            step
            for i in (2 * t, 2 * t + 1)
            for step in gathering(cells, land_idx, direction(i), landed.at[i], 80)
        )
        for x in range(x0, x0 + CX // 4, 2):
            left, right = [], []
            for y in (x, x + 1):
                z = zlines[y]
                shifted = zlines[y + 1] + jnp.where(final, 0.0, pltpu.roll(z, 127, 1))
                half_image = (2.0 + 0.5 * coef[y : y + 1, :]) * z - shifted
                left.append(zparts[y])
                right.append(stacked(half_image))
            total = total + lax.dot_general(
                jnp.concatenate(left, axis=1),
                jnp.concatenate(right, axis=1),
                (((1,), (1,)), ((), ())),
                preferred_element_type=f32,
            )
            next(beside, None)
        finish(beside)
        return total

    def put(slot, block):
        gap = jnp.zeros((HALF, 64 - K), f32)
        held[x_me * 9 + slot] = jnp.concatenate([block[:HALF], gap, block[HALF:], gap], axis=1)

    def x_copy(g, k):
        span = pl.ds(x_me * 9 + GROUPS[g][0], GROUPS[g][1])
        return pltpu.make_async_remote_copy(
            src_ref=held.at[span],
            dst_ref=held.at[span],
            send_sem=x_send.at[g * 3 + k - 1],
            recv_sem=x_recv.at[g * 3 + k - 1],
            device_id=(row, lax.rem(col + NZ * k, NCOL)),
            device_id_type=MESH,
        )

    def pair(t):
        for i in (2 * t, 2 * t + 1):
            dr, dc = STEPS[i]
            if remote:
                @pl.when(inside(-dr, -dc))
                def _():
                    near_copy(i, dr, dc).wait_recv()
            product = jnp.dot(
                stacked(arrived[i]), landed[i].astype(bf16), preferred_element_type=f32
            )
            put(SLOTS[i], unstack(product.T))

    def send_along_x(g):
        if remote:
            for k in (2, 1, 3):
                x_copy(g, k).start()

    own = land(0, 0, jnp.zeros((2 * K, 2 * K), f32))
    own = land(2, CX // 4, own)
    pair(0)
    send_along_x(0)
    own = land(1, CX // 2, own)
    pair(2)
    send_along_x(1)
    own = land(3, 3 * CX // 4, own)
    own = unstack(own)
    put(OWN_SLOT, own + own.T)
    pair(1)
    send_along_x(2)
    pair(3)
    send_along_x(3)

    pick_copy.wait()
    if remote:
        for g in range(4):
            for k in range(1, 4):
                x_copy(g, k).wait_recv()

    def z_copy(k):
        return pltpu.make_async_remote_copy(
            src_ref=strips.at[k],
            dst_ref=received.at[z_me],
            send_sem=z_send.at[k - 1],
            recv_sem=z_recv.at[k - 1],
            device_id=(row, x_me * NZ + lax.rem(z_me + k, NZ)),
            device_id_type=MESH,
        )

    for k in (2, 1, 3, 0):
        target = lax.rem(z_me + k, NZ)
        found = [held[pick[target * 8 + m, 0]] for m in range(8)]
        upper = jnp.concatenate([block[:, 0:K] for block in found], axis=1)
        lower = jnp.concatenate([block[:, 64 : 64 + K] for block in found], axis=1)
        strip = jnp.concatenate([upper, lower], axis=0)
        if k:
            strips[k] = strip
            if remote:
                z_copy(k).start()
        else:
            received[z_me] = strip

    if remote:
        for i, (dr, dc) in enumerate(STEPS):
            @pl.when(inside(dr, dc))
            def _():
                near_copy(i, dr, dc).wait_send()
        for g in range(4):
            for k in range(1, 4):
                x_copy(g, k).wait_send()
        for k in range(1, 4):
            z_copy(k).wait_send()
        for k in range(1, 4):
            z_copy(k).wait_recv()
    strips_out[...] = received[...]


def place_strips(strips, mask, out):
    for p in range(NCOL):
        keep = mask[p : p + 1, :] > 0.5
        out[p * K : (p + 1) * K, :] = jnp.where(keep, strips[p % NZ], 0.0)


def assemble_call(remote, *args):
    vmem = pl.BlockSpec(memory_space=pltpu.VMEM)
    hbm = pl.BlockSpec(memory_space=pl.ANY)
    dma = pltpu.SemaphoreType.DMA
    return pl.pallas_call(
        functools.partial(assemble, remote),
        out_shape=(
            jax.ShapeDtypeStruct((NZ, K, WIDE), f32),
            jax.ShapeDtypeStruct((NCOL, WIDE), f32),
        ),
        in_specs=[hbm] * 7,
        out_specs=(vmem, vmem),
        scratch_shapes=[
            pltpu.VMEM((CX + 1, K, 128), f32),
            pltpu.VMEM((CX, 2 * K, 128), bf16),
            pltpu.VMEM((CX * 128, 128), f32),
            pltpu.VMEM((8, ROWS, ROWS), f32),
            pltpu.VMEM((ROWS, 128), f32),
            pltpu.VMEM((ROWS, 128), f32),
            pltpu.VMEM((2 * K, ROWS), bf16),
            pltpu.VMEM((2 * K, ROWS), bf16),
            pltpu.VMEM((8, ROWS, 128), f32),
            pltpu.VMEM((8, K, ROWS), f32),
            pltpu.VMEM((8, K, ROWS), f32),
            pltpu.VMEM((EMPTY + 1, HALF, 128), f32),
            pltpu.VMEM((NZ, K, WIDE), f32),
            pltpu.VMEM((NZ, K, WIDE), f32),
            pltpu.VMEM((CX, 128), f32),
            pltpu.VMEM((128,), jnp.int32),
            pltpu.VMEM((32, 128), jnp.int32),
            pltpu.SMEM((8, ROWS), jnp.int32),
            pltpu.SMEM((8, ROWS), jnp.int32),
            pltpu.SMEM((1, 8), jnp.int32),
            pltpu.SMEM((32, 128), jnp.int32),
            dma((HALVES,)), dma((8,)), dma, dma, dma((3,)), dma,
            dma((8,)), dma((8,)), dma((12,)), dma((12,)), dma((3,)), dma((3,)),
        ],
        compiler_params=pltpu.CompilerParams(
            collective_id=0 if remote else None,
            has_side_effects=True,
            vmem_limit_bytes=56 * 2**20,
        ),
        cost_estimate=pl.CostEstimate(
            flops=2 * 10**9, bytes_accessed=18 * 10**6, transcendentals=0
        ),
    )(*args)


def on_device(zvecs, coef, blocks, send_idx, land_idx, active, order):
    strips, mask = assemble_call(True, zvecs, coef, blocks, send_idx, land_idx, active, order)
    return pl.pallas_call(
        place_strips,
        out_shape=jax.ShapeDtypeStruct((NCOL * K, WIDE), f32),
        in_specs=[pl.BlockSpec(memory_space=pltpu.VMEM)] * 2,
        out_specs=pl.BlockSpec(memory_space=pltpu.VMEM),
    )(strips, mask)


def solution(mesh):
    in_specs = (
        P("row", "col", None, None, None),
        P("row", "col", None, None),
        P("row", "col", None, None, None),
        P("row", "col", None, None),
        P("row", "col", None, None),
        P("row", "col", None),
        P(),
    )
    return jax.shard_map(
        on_device, mesh=mesh, in_specs=in_specs, out_specs=P("row", "col"), check_vma=False
    )
```

```python
import functools

import jax
import jax.numpy as jnp
from jax import lax
from jax.experimental import pallas as pl
from jax.experimental.pallas import tpu as pltpu
from jax.sharding import PartitionSpec as P

f32 = jnp.float32
bf16 = jnp.bfloat16
MESH = pl.DeviceIdType.MESH

K = 48
CX = 128
ROWS = 640
NROW = 8
NCOL = 16
NX = 4
NZ = 4
PARTS = 2
PER = CX // PARTS
TURN = 32
HALF = K // 2
WIDE = 8 * K
STEPS = ((-1, 1), (-1, -1), (0, 1), (0, -1), (-1, 0), (1, 0), (1, 1), (1, -1))
GROUPS = ((0, 2), (2, 2), (4, 3), (7, 2))
SLOTS = (0, 1, 5, 6, 2, 3, 7, 8)
OWN_SLOT = 4
EMPTY = NX * 9


def split(x):
    high = x.astype(bf16)
    return high, (x - high.astype(f32)).astype(bf16)


def stacked(x):
    return jnp.concatenate(split(x), axis=0)


def unstack(product):
    return product[:K, :K] + product[K : 2 * K, :K] + product[:K, K : 2 * K]


def direction(i):
    nine = (STEPS[i][0] + 1) * 3 + STEPS[i][1] + 1
    return nine - nine // 5


def gathering(cells, index, n, rows, batch):
    for j in range(ROWS):
        rows[pl.ds(j, 1), :] = cells[pl.ds(index[n, j], 1), :]
        if j % batch == batch - 1:
            yield


def finish(steps):
    for _ in steps:
        pass


def times_block(picked, block, factor, out, beside):
    for q0 in range(0, ROWS, 256):
        q1 = min(q0 + 256, ROWS)
        total, low_total = None, None
        for p0 in range(0, ROWS, 256):
            p1 = min(p0 + 256, ROWS)
            high, low = split(block[p0:p1, q0:q1])
            one = jnp.dot(picked[:, p0:p1], high, preferred_element_type=f32)
            two = jnp.dot(picked[0:K, p0:p1], low, preferred_element_type=f32)
            total = one if total is None else total + one
            low_total = two if low_total is None else low_total + two
            next(beside, None)
        out[:, q0:q1] = (total[0:K] + total[K : 2 * K] + low_total) * factor
    finish(beside)


def assemble(
    remote,
    z_hbm, coef_hbm, blocks_hbm, send_hbm, land_hbm, active_hbm, order_hbm,
    strips_out, mask_out,
    zlines, zparts, cells, blocks, rows_a, rows_b, picked_a, picked_b, landed, sent, arrived,
    held, strips, mask, coef, order,
    pick_vec, send_idx, land_idx, active, pick,
    z_sem, block_sem, send_idx_sem, land_idx_sem, small_sem, pick_sem, out_sem,
    near_send, near_recv, x_send, x_recv, z_send, z_recv,
):
    row = lax.axis_index("row") if remote else 3
    col = lax.axis_index("col") if remote else 5
    x_me = col // NZ
    z_me = lax.rem(col, NZ)

    def lines_of(part):
        return zlines.at[pl.ds(part * PER, PER)]

    send_copy = pltpu.make_async_copy(send_hbm.at[0, 0], send_idx, send_idx_sem)
    send_copy.start()
    for part in range(PARTS):
        for k in range(K):
            pltpu.make_async_copy(
                z_hbm.at[0, 0, k, pl.ds(part * PER, PER), :],
                zlines.at[pl.ds(part * PER, PER), k, :],
                z_sem.at[part],
            ).start()
    active_copy = pltpu.make_async_copy(active_hbm.at[0], active, small_sem.at[0])
    active_copy.start()
    coef_copy = pltpu.make_async_copy(coef_hbm.at[0, 0], coef, small_sem.at[1])
    order_copy = pltpu.make_async_copy(order_hbm, order, small_sem.at[2])
    land_copy = pltpu.make_async_copy(land_hbm.at[0, 0], land_idx, land_idx_sem)
    block_copies = [
        pltpu.make_async_copy(blocks_hbm.at[0, 0, direction(i)], blocks.at[i], block_sem.at[i])
        for i in range(8)
    ]

    if remote:
        barrier = pltpu.get_barrier_semaphore()
        for dr, dc in STEPS:
            peer = (lax.rem(row + dr + NROW, NROW), lax.rem(col + dc + NCOL, NCOL))
            pl.semaphore_signal(barrier, inc=1, device_id=peer, device_id_type=MESH)
        for k in range(1, 4):
            peer = (row, lax.rem(col + NZ * k, NCOL))
            pl.semaphore_signal(barrier, inc=1, device_id=peer, device_id_type=MESH)
            peer = (row, x_me * NZ + lax.rem(z_me + k, NZ))
            pl.semaphore_signal(barrier, inc=1, device_id=peer, device_id_type=MESH)

    zlines[CX] = jnp.zeros((K, 128), f32)
    def turn_chunk(i, carry):
        for u in range(TURN):
            both = stacked(zlines[i * TURN + u])
            zparts[i * TURN + u] = both
            cells[pl.ds((i * TURN + u) * 128, 128), 0 : 2 * K] = both.T.astype(f32)
        return carry

    for part in range(PARTS):
        pltpu.make_async_copy(lines_of(part), lines_of(part), z_sem.at[part]).wait()
        if part == PARTS - 1:
            for copy in block_copies + [order_copy, coef_copy, land_copy]:
                copy.start()
        lax.fori_loop(part * PER // TURN, (part + 1) * PER // TURN, turn_chunk, 0)

    send_copy.wait()
    active_copy.wait()

    if remote:
        pl.semaphore_wait(barrier, 14)

    def near_copy(i, dr, dc):
        peer = (row + dr, col + dc)
        return pltpu.make_async_remote_copy(
            src_ref=sent.at[i],
            dst_ref=arrived.at[i],
            send_sem=near_send.at[i],
            recv_sem=near_recv.at[i],
            device_id=peer,
            device_id_type=MESH,
        )

    def inside(dr, dc):
        r, c = row + dr, col + dc
        return (r >= 0) & (r < NROW) & (c >= 0) & (c < NCOL)

    rows = (rows_a, rows_b)
    picked = (picked_a, picked_b)

    def pick_up(i):
        return gathering(cells, send_idx, direction(i), rows[i % 2], 72)

    def flip(i):
        picked[i % 2][...] = rows[i % 2][...].astype(bf16).T[0 : 2 * K]

    def multiply(i, beside=iter(())):
        block_copies[i].wait()
        keep = jnp.where(active[0, direction(i)] == 1, 1.0, 0.0)
        times_block(picked[i % 2], blocks.at[i], keep, sent.at[i], beside)
        if remote:
            dr, dc = STEPS[i]

            @pl.when(inside(dr, dc))
            def _():
                near_copy(i, dr, dc).start()

    finish(pick_up(0))
    flip(0)
    multiply(0)
    finish(pick_up(1))
    flip(1)
    for i in range(1, 7):
        multiply(i, pick_up(i + 1))
        flip(i + 1)
    multiply(7)

    order_copy.wait()
    lane = lax.broadcasted_iota(jnp.int32, (32, 128), 1)
    line = lax.broadcasted_iota(jnp.int32, (32, 128), 0)
    owner = order[...].reshape(1, 128)
    source = jnp.sum(
        jnp.where(owner == x_me * 32 + line, lane, 0), axis=1, keepdims=True
    )
    from_row = source // NCOL
    from_col = source - from_row * NCOL
    turn = (z_me - from_col + NCOL) % NZ
    dr = row - from_row
    dc = jnp.where(turn == 3, -1, turn)
    to_col = from_col + dc
    step = 2 * (dr + 1) + jnp.where(dc < 0, 1, 0)
    slot = jnp.where(
        dc == 0,
        jnp.where(dr == 0, OWN_SLOT, jnp.where(dr < 0, 2, 3)),
        step + jnp.where(step >= 2, 3, 0),
    )
    good = (turn != 2) & (to_col >= 0) & (to_col < NCOL) & (dr >= -1) & (dr <= 1)
    place = jnp.where(good, (to_col // NZ) * 9 + slot, EMPTY)
    pick_vec[...] = jnp.broadcast_to(place, (32, 128))
    pick_copy = pltpu.make_async_copy(pick_vec, pick, pick_sem)
    pick_copy.start()

    lane8 = lax.broadcasted_iota(jnp.int32, (8, 128), 1)
    line8 = lax.broadcasted_iota(jnp.int32, (8, 128), 0)
    mine = jnp.sum(jnp.where(owner == col * 8 + line8, lane8, 0), axis=1, keepdims=True)
    at = lax.broadcasted_iota(jnp.int32, (8, WIDE), 1) // K
    here = at == lax.broadcasted_iota(jnp.int32, (8, WIDE), 0)
    mine = jnp.sum(jnp.where(here, jnp.broadcast_to(mine, (8, WIDE)), 0), axis=0, keepdims=True)
    mine_row = mine // NCOL
    mine_col = mine - mine_row * NCOL
    column = lax.broadcasted_iota(jnp.int32, (NCOL, WIDE), 0)
    near = (jnp.abs(mine_col - column) <= 1) & (jnp.abs(mine_row - row) <= 1)

    mask[...] = jnp.where(near, 1.0, 0.0)
    mask_copy = pltpu.make_async_copy(mask, mask_out, out_sem.at[0])
    mask_copy.start()
    held[EMPTY] = jnp.zeros((HALF, 128), f32)

    land_copy.wait()
    coef_copy.wait()
    final = lax.broadcasted_iota(jnp.int32, (K, 128), 1) == 127

    def land(t, x0, total):
        beside = (
            step
            for i in (2 * t, 2 * t + 1)
            for step in gathering(cells, land_idx, direction(i), landed.at[i], 80)
        )
        for x in range(x0, x0 + CX // 4, 2):
            left, right = [], []
            for y in (x, x + 1):
                z = zlines[y]
                shifted = zlines[y + 1] + jnp.where(final, 0.0, pltpu.roll(z, 127, 1))
                half_image = (2.0 + 0.5 * coef[y : y + 1, :]) * z - shifted
                left.append(zparts[y])
                right.append(stacked(half_image))
            total = total + lax.dot_general(
                jnp.concatenate(left, axis=1),
                jnp.concatenate(right, axis=1),
                (((1,), (1,)), ((), ())),
                preferred_element_type=f32,
            )
            next(beside, None)
        finish(beside)
        return total

    def put(slot, block):
        gap = jnp.zeros((HALF, 64 - K), f32)
        held[x_me * 9 + slot] = jnp.concatenate([block[:HALF], gap, block[HALF:], gap], axis=1)

    def x_copy(g, k):
        span = pl.ds(x_me * 9 + GROUPS[g][0], GROUPS[g][1])
        return pltpu.make_async_remote_copy(
            src_ref=held.at[span],
            dst_ref=held.at[span],
            send_sem=x_send.at[g * 3 + k - 1],
            recv_sem=x_recv.at[g * 3 + k - 1],
            device_id=(row, lax.rem(col + NZ * k, NCOL)),
            device_id_type=MESH,
        )

    def pair(t):
        for i in (2 * t, 2 * t + 1):
            dr, dc = STEPS[i]
            if remote:
                @pl.when(inside(-dr, -dc))
                def _():
                    near_copy(i, dr, dc).wait_recv()
            product = jnp.dot(
                stacked(arrived[i]), landed[i].astype(bf16), preferred_element_type=f32
            )
            put(SLOTS[i], unstack(product.T))

    def send_along_x(g):
        if remote:
            for k in (2, 1, 3):
                x_copy(g, k).start()

    own = land(0, 0, jnp.zeros((2 * K, 2 * K), f32))
    own = land(2, CX // 4, own)
    pair(0)
    send_along_x(0)
    own = land(1, CX // 2, own)
    pair(2)
    send_along_x(1)
    own = land(3, 3 * CX // 4, own)
    own = unstack(own)
    put(OWN_SLOT, own + own.T)
    pair(1)
    send_along_x(2)
    pair(3)
    send_along_x(3)

    pick_copy.wait()
    if remote:
        for g in range(4):
            for k in range(1, 4):
                x_copy(g, k).wait_recv()

    def z_copy(k):
        return pltpu.make_async_remote_copy(
            src_ref=strips.at[k],
            dst_ref=strips_out.at[z_me],
            send_sem=z_send.at[k - 1],
            recv_sem=z_recv.at[k - 1],
            device_id=(row, x_me * NZ + lax.rem(z_me + k, NZ)),
            device_id_type=MESH,
        )

    for k in (2, 1, 3, 0):
        target = lax.rem(z_me + k, NZ)
        found = [held[pick[target * 8 + m, 0]] for m in range(8)]
        upper = jnp.concatenate([block[:, 0:K] for block in found], axis=1)
        lower = jnp.concatenate([block[:, 64 : 64 + K] for block in found], axis=1)
        strip = jnp.concatenate([upper, lower], axis=0)
        strips[k] = strip
        if k and remote:
            z_copy(k).start()
    own_copy = pltpu.make_async_copy(strips.at[0], strips_out.at[z_me], out_sem.at[1])
    own_copy.start()

    if remote:
        for i, (dr, dc) in enumerate(STEPS):
            @pl.when(inside(dr, dc))
            def _():
                near_copy(i, dr, dc).wait_send()
        for g in range(4):
            for k in range(1, 4):
                x_copy(g, k).wait_send()
        for k in range(1, 4):
            z_copy(k).wait_send()
        for k in range(1, 4):
            z_copy(k).wait_recv()
    mask_copy.wait()
    own_copy.wait()


def place_strips(strips, mask, out):
    for p in range(NCOL):
        keep = mask[p : p + 1, :] > 0.5
        out[p * K : (p + 1) * K, :] = jnp.where(keep, strips[p % NZ], 0.0)


def assemble_call(remote, *args):
    hbm = pl.BlockSpec(memory_space=pl.ANY)
    dma = pltpu.SemaphoreType.DMA
    return pl.pallas_call(
        functools.partial(assemble, remote),
        out_shape=(
            jax.ShapeDtypeStruct((NZ, K, WIDE), f32),
            jax.ShapeDtypeStruct((NCOL, WIDE), f32),
        ),
        in_specs=[hbm] * 7,
        out_specs=(hbm, hbm),
        scratch_shapes=[
            pltpu.VMEM((CX + 1, K, 128), f32),
            pltpu.VMEM((CX, 2 * K, 128), bf16),
            pltpu.VMEM((CX * 128, 128), f32),
            pltpu.VMEM((8, ROWS, ROWS), f32),
            pltpu.VMEM((ROWS, 128), f32),
            pltpu.VMEM((ROWS, 128), f32),
            pltpu.VMEM((2 * K, ROWS), bf16),
            pltpu.VMEM((2 * K, ROWS), bf16),
            pltpu.VMEM((8, ROWS, 128), f32),
            pltpu.VMEM((8, K, ROWS), f32),
            pltpu.VMEM((8, K, ROWS), f32),
            pltpu.VMEM((EMPTY + 1, HALF, 128), f32),
            pltpu.VMEM((NZ, K, WIDE), f32),
            pltpu.VMEM((NCOL, WIDE), f32),
            pltpu.VMEM((CX, 128), f32),
            pltpu.VMEM((128,), jnp.int32),
            pltpu.VMEM((32, 128), jnp.int32),
            pltpu.SMEM((8, ROWS), jnp.int32),
            pltpu.SMEM((8, ROWS), jnp.int32),
            pltpu.SMEM((1, 8), jnp.int32),
            pltpu.SMEM((32, 128), jnp.int32),
            dma((PARTS,)), dma((8,)), dma, dma, dma((3,)), dma, dma((2,)),
            dma((8,)), dma((8,)), dma((12,)), dma((12,)), dma((3,)), dma((3,)),
        ],
        compiler_params=pltpu.CompilerParams(
            collective_id=0 if remote else None,
            has_side_effects=True,
            vmem_limit_bytes=56 * 2**20,
        ),
        cost_estimate=pl.CostEstimate(
            flops=2 * 10**9, bytes_accessed=18 * 10**6, transcendentals=0
        ),
    )(*args)


def on_device(zvecs, coef, blocks, send_idx, land_idx, active, order):
    strips, mask = assemble_call(True, zvecs, coef, blocks, send_idx, land_idx, active, order)
    return pl.pallas_call(
        place_strips,
        out_shape=jax.ShapeDtypeStruct((NCOL * K, WIDE), f32),
        in_specs=[pl.BlockSpec(memory_space=pltpu.VMEM)] * 2,
        out_specs=pl.BlockSpec(memory_space=pltpu.VMEM),
    )(strips, mask)


def solution(mesh):
    in_specs = (
        P("row", "col", None, None, None),
        P("row", "col", None, None),
        P("row", "col", None, None, None),
        P("row", "col", None, None),
        P("row", "col", None, None),
        P("row", "col", None),
        P(),
    )
    return jax.shard_map(
        on_device, mesh=mesh, in_specs=in_specs, out_specs=P("row", "col"), check_vma=False
    )
```

```python
import functools

import jax
import jax.numpy as jnp
from jax import lax
from jax.experimental import pallas as pl
from jax.experimental.pallas import tpu as pltpu
from jax.sharding import PartitionSpec as P

f32 = jnp.float32
bf16 = jnp.bfloat16
MESH = pl.DeviceIdType.MESH

K = 48
CX = 128
ROWS = 640
NROW = 8
NCOL = 16
NX = 4
NZ = 4
PARTS = 2
PER = CX // PARTS
TURN = 32
HALF = K // 2
WIDE = 8 * K
STEPS = ((-1, 1), (-1, -1), (0, 1), (0, -1), (-1, 0), (1, 0), (1, 1), (1, -1))
GROUPS = ((0, 2), (2, 2), (4, 3), (7, 2))
SLOTS = (0, 1, 5, 6, 2, 3, 7, 8)
OWN_SLOT = 4
EMPTY = NX * 9


def split(x):
    high = x.astype(bf16)
    return high, (x - high.astype(f32)).astype(bf16)


def stacked(x):
    return jnp.concatenate(split(x), axis=0)


def unstack(product):
    return product[:K, :K] + product[K : 2 * K, :K] + product[:K, K : 2 * K]


def direction(i):
    nine = (STEPS[i][0] + 1) * 3 + STEPS[i][1] + 1
    return nine - nine // 5


def gathering(cells, index, n, rows, batch):
    for j in range(ROWS):
        rows[pl.ds(j, 1), :] = cells[pl.ds(index[n, j], 1), :]
        if j % batch == batch - 1:
            yield


def finish(steps):
    for _ in steps:
        pass


def times_block(picked, block, factor, out, beside):
    for q0 in range(0, ROWS, 256):
        q1 = min(q0 + 256, ROWS)
        total, low_total = None, None
        for p0 in range(0, ROWS, 256):
            p1 = min(p0 + 256, ROWS)
            high, low = split(block[p0:p1, q0:q1])
            one = jnp.dot(picked[:, p0:p1], high, preferred_element_type=f32)
            two = jnp.dot(picked[0:K, p0:p1], low, preferred_element_type=f32)
            total = one if total is None else total + one
            low_total = two if low_total is None else low_total + two
            next(beside, None)
        out[:, q0:q1] = (total[0:K] + total[K : 2 * K] + low_total) * factor
    finish(beside)


def assemble(
    remote,
    z_hbm, coef_hbm, blocks_hbm, send_hbm, land_hbm, active_hbm, order_hbm,
    strips_out, mask_out,
    zlines, zparts, cells, blocks, rows_a, rows_b, picked_a, picked_b, landed, sent, arrived,
    held, strips, mask, coef, order,
    pick_vec, send_idx, land_idx, active, pick,
    z_sem, block_sem, send_idx_sem, land_idx_sem, small_sem, pick_sem, out_sem,
    near_send, near_recv, x_send, x_recv, z_send, z_recv,
):
    row = lax.axis_index("row") if remote else 3
    col = lax.axis_index("col") if remote else 5
    x_me = col // NZ
    z_me = lax.rem(col, NZ)

    def lines_of(part):
        return zlines.at[pl.ds(part * PER, PER)]

    send_copy = pltpu.make_async_copy(send_hbm.at[0, 0], send_idx, send_idx_sem)
    send_copy.start()
    for part in range(PARTS):
        for k in range(K):
            pltpu.make_async_copy(
                z_hbm.at[0, 0, k, pl.ds(part * PER, PER), :],
                zlines.at[pl.ds(part * PER, PER), k, :],
                z_sem.at[part],
            ).start()
    active_copy = pltpu.make_async_copy(active_hbm.at[0], active, small_sem.at[0])
    active_copy.start()
    coef_copy = pltpu.make_async_copy(coef_hbm.at[0, 0], coef, small_sem.at[1])
    order_copy = pltpu.make_async_copy(order_hbm, order, small_sem.at[2])
    land_copy = pltpu.make_async_copy(land_hbm.at[0, 0], land_idx, land_idx_sem)
    block_copies = [
        pltpu.make_async_copy(blocks_hbm.at[0, 0, direction(i)], blocks.at[i], block_sem.at[i])
        for i in range(8)
    ]

    if remote:
        barrier = pltpu.get_barrier_semaphore()
        for dr, dc in STEPS:
            peer = (lax.rem(row + dr + NROW, NROW), lax.rem(col + dc + NCOL, NCOL))
            pl.semaphore_signal(barrier, inc=1, device_id=peer, device_id_type=MESH)
        for k in range(1, 4):
            peer = (row, lax.rem(col + NZ * k, NCOL))
            pl.semaphore_signal(barrier, inc=1, device_id=peer, device_id_type=MESH)
            peer = (row, x_me * NZ + lax.rem(z_me + k, NZ))
            pl.semaphore_signal(barrier, inc=1, device_id=peer, device_id_type=MESH)

    zlines[CX] = jnp.zeros((K, 128), f32)
    def turn_chunk(i, carry):
        for u in range(TURN):
            both = stacked(zlines[i * TURN + u])
            zparts[i * TURN + u] = both
            cells[pl.ds((i * TURN + u) * 128, 128), 0 : 2 * K] = both.T.astype(f32)
        return carry

    for part in range(PARTS):
        pltpu.make_async_copy(lines_of(part), lines_of(part), z_sem.at[part]).wait()
        if part == PARTS - 1:
            for copy in block_copies + [order_copy, coef_copy, land_copy]:
                copy.start()
        lax.fori_loop(part * PER // TURN, (part + 1) * PER // TURN, turn_chunk, 0)

    send_copy.wait()
    active_copy.wait()

    if remote:
        pl.semaphore_wait(barrier, 14)

    def near_copy(i, dr, dc):
        peer = (row + dr, col + dc)
        return pltpu.make_async_remote_copy(
            src_ref=sent.at[i],
            dst_ref=arrived.at[i],
            send_sem=near_send.at[i],
            recv_sem=near_recv.at[i],
            device_id=peer,
            device_id_type=MESH,
        )

    def inside(dr, dc):
        r, c = row + dr, col + dc
        return (r >= 0) & (r < NROW) & (c >= 0) & (c < NCOL)

    rows = (rows_a, rows_b)
    picked = (picked_a, picked_b)

    def pick_up(i):
        return gathering(cells, send_idx, direction(i), rows[i % 2], 72)

    def flip(i):
        picked[i % 2][...] = rows[i % 2][...].astype(bf16).T[0 : 2 * K]

    def multiply(i, beside=iter(())):
        block_copies[i].wait()
        keep = jnp.where(active[0, direction(i)] == 1, 1.0, 0.0)
        times_block(picked[i % 2], blocks.at[i], keep, sent.at[i], beside)
        if remote:
            dr, dc = STEPS[i]

            @pl.when(inside(dr, dc))
            def _():
                near_copy(i, dr, dc).start()

    finish(pick_up(0))
    flip(0)
    multiply(0)
    finish(pick_up(1))
    flip(1)
    for i in range(1, 7):
        multiply(i, pick_up(i + 1))
        flip(i + 1)
    multiply(7)

    land_copy.wait()
    coef_copy.wait()
    final = lax.broadcasted_iota(jnp.int32, (K, 128), 1) == 127

    def land(t, x0, total):
        beside = (
            step
            for i in (2 * t, 2 * t + 1)
            for step in gathering(cells, land_idx, direction(i), landed.at[i], 80)
        )
        for x in range(x0, x0 + CX // 4, 2):
            left, right = [], []
            for y in (x, x + 1):
                z = zlines[y]
                shifted = zlines[y + 1] + jnp.where(final, 0.0, pltpu.roll(z, 127, 1))
                half_image = (2.0 + 0.5 * coef[y : y + 1, :]) * z - shifted
                left.append(zparts[y])
                right.append(stacked(half_image))
            total = total + lax.dot_general(
                jnp.concatenate(left, axis=1),
                jnp.concatenate(right, axis=1),
                (((1,), (1,)), ((), ())),
                preferred_element_type=f32,
            )
            next(beside, None)
        finish(beside)
        return total

    def put(slot, block):
        gap = jnp.zeros((HALF, 64 - K), f32)
        held[x_me * 9 + slot] = jnp.concatenate([block[:HALF], gap, block[HALF:], gap], axis=1)

    def x_copy(g, k):
        span = pl.ds(x_me * 9 + GROUPS[g][0], GROUPS[g][1])
        return pltpu.make_async_remote_copy(
            src_ref=held.at[span],
            dst_ref=held.at[span],
            send_sem=x_send.at[g * 3 + k - 1],
            recv_sem=x_recv.at[g * 3 + k - 1],
            device_id=(row, lax.rem(col + NZ * k, NCOL)),
            device_id_type=MESH,
        )

    def pair(t):
        for i in (2 * t, 2 * t + 1):
            dr, dc = STEPS[i]
            if remote:
                @pl.when(inside(-dr, -dc))
                def _():
                    near_copy(i, dr, dc).wait_recv()
            product = jnp.dot(
                stacked(arrived[i]), landed[i].astype(bf16), preferred_element_type=f32
            )
            put(SLOTS[i], unstack(product.T))

    def send_along_x(g):
        if remote:
            for k in (2, 1, 3):
                x_copy(g, k).start()

    own = land(0, 0, jnp.zeros((2 * K, 2 * K), f32))
    own = land(2, CX // 4, own)
    pair(0)
    send_along_x(0)
    own = land(1, CX // 2, own)
    pair(2)
    send_along_x(1)
    own = land(3, 3 * CX // 4, own)
    own = unstack(own)
    put(OWN_SLOT, own + own.T)
    pair(1)
    send_along_x(2)
    pair(3)
    send_along_x(3)

    order_copy.wait()
    lane = lax.broadcasted_iota(jnp.int32, (32, 128), 1)
    line = lax.broadcasted_iota(jnp.int32, (32, 128), 0)
    owner = order[...].reshape(1, 128)
    source = jnp.sum(
        jnp.where(owner == x_me * 32 + line, lane, 0), axis=1, keepdims=True
    )
    from_row = source // NCOL
    from_col = source - from_row * NCOL
    turn = (z_me - from_col + NCOL) % NZ
    dr = row - from_row
    dc = jnp.where(turn == 3, -1, turn)
    to_col = from_col + dc
    step = 2 * (dr + 1) + jnp.where(dc < 0, 1, 0)
    slot = jnp.where(
        dc == 0,
        jnp.where(dr == 0, OWN_SLOT, jnp.where(dr < 0, 2, 3)),
        step + jnp.where(step >= 2, 3, 0),
    )
    good = (turn != 2) & (to_col >= 0) & (to_col < NCOL) & (dr >= -1) & (dr <= 1)
    place = jnp.where(good, (to_col // NZ) * 9 + slot, EMPTY)
    pick_vec[...] = jnp.broadcast_to(place, (32, 128))
    pick_copy = pltpu.make_async_copy(pick_vec, pick, pick_sem)
    pick_copy.start()

    held[EMPTY] = jnp.zeros((HALF, 128), f32)

    pick_copy.wait()
    if remote:
        for g in range(4):
            for k in range(1, 4):
                x_copy(g, k).wait_recv()

    def z_copy(k):
        return pltpu.make_async_remote_copy(
            src_ref=strips.at[k],
            dst_ref=strips_out.at[z_me],
            send_sem=z_send.at[k - 1],
            recv_sem=z_recv.at[k - 1],
            device_id=(row, x_me * NZ + lax.rem(z_me + k, NZ)),
            device_id_type=MESH,
        )

    for k in (2, 1, 3, 0):
        target = lax.rem(z_me + k, NZ)
        found = [held[pick[target * 8 + m, 0]] for m in range(8)]
        upper = jnp.concatenate([block[:, 0:K] for block in found], axis=1)
        lower = jnp.concatenate([block[:, 64 : 64 + K] for block in found], axis=1)
        strip = jnp.concatenate([upper, lower], axis=0)
        strips[k] = strip
        if k and remote:
            z_copy(k).start()
    own_copy = pltpu.make_async_copy(strips.at[0], strips_out.at[z_me], out_sem.at[1])
    own_copy.start()

    lane8 = lax.broadcasted_iota(jnp.int32, (8, 128), 1)
    line8 = lax.broadcasted_iota(jnp.int32, (8, 128), 0)
    mine = jnp.sum(jnp.where(owner == col * 8 + line8, lane8, 0), axis=1, keepdims=True)
    at = lax.broadcasted_iota(jnp.int32, (8, WIDE), 1) // K
    here = at == lax.broadcasted_iota(jnp.int32, (8, WIDE), 0)
    mine = jnp.sum(jnp.where(here, jnp.broadcast_to(mine, (8, WIDE)), 0), axis=0, keepdims=True)
    mine_row = mine // NCOL
    mine_col = mine - mine_row * NCOL
    column = lax.broadcasted_iota(jnp.int32, (NCOL, WIDE), 0)
    near = (jnp.abs(mine_col - column) <= 1) & (jnp.abs(mine_row - row) <= 1)

    mask[...] = jnp.where(near, 1.0, 0.0)
    mask_copy = pltpu.make_async_copy(mask, mask_out, out_sem.at[0])
    mask_copy.start()
    if remote:
        for i, (dr, dc) in enumerate(STEPS):
            @pl.when(inside(dr, dc))
            def _():
                near_copy(i, dr, dc).wait_send()
        for g in range(4):
            for k in range(1, 4):
                x_copy(g, k).wait_send()
        for k in range(1, 4):
            z_copy(k).wait_send()
        for k in range(1, 4):
            z_copy(k).wait_recv()
    mask_copy.wait()
    own_copy.wait()


def place_strips(strips, mask, out):
    for p in range(NCOL):
        keep = mask[p : p + 1, :] > 0.5
        out[p * K : (p + 1) * K, :] = jnp.where(keep, strips[p % NZ], 0.0)


def assemble_call(remote, *args):
    hbm = pl.BlockSpec(memory_space=pl.ANY)
    dma = pltpu.SemaphoreType.DMA
    return pl.pallas_call(
        functools.partial(assemble, remote),
        out_shape=(
            jax.ShapeDtypeStruct((NZ, K, WIDE), f32),
            jax.ShapeDtypeStruct((NCOL, WIDE), f32),
        ),
        in_specs=[hbm] * 7,
        out_specs=(hbm, hbm),
        scratch_shapes=[
            pltpu.VMEM((CX + 1, K, 128), f32),
            pltpu.VMEM((CX, 2 * K, 128), bf16),
            pltpu.VMEM((CX * 128, 128), f32),
            pltpu.VMEM((8, ROWS, ROWS), f32),
            pltpu.VMEM((ROWS, 128), f32),
            pltpu.VMEM((ROWS, 128), f32),
            pltpu.VMEM((2 * K, ROWS), bf16),
            pltpu.VMEM((2 * K, ROWS), bf16),
            pltpu.VMEM((8, ROWS, 128), f32),
            pltpu.VMEM((8, K, ROWS), f32),
            pltpu.VMEM((8, K, ROWS), f32),
            pltpu.VMEM((EMPTY + 1, HALF, 128), f32),
            pltpu.VMEM((NZ, K, WIDE), f32),
            pltpu.VMEM((NCOL, WIDE), f32),
            pltpu.VMEM((CX, 128), f32),
            pltpu.VMEM((128,), jnp.int32),
            pltpu.VMEM((32, 128), jnp.int32),
            pltpu.SMEM((8, ROWS), jnp.int32),
            pltpu.SMEM((8, ROWS), jnp.int32),
            pltpu.SMEM((1, 8), jnp.int32),
            pltpu.SMEM((32, 128), jnp.int32),
            dma((PARTS,)), dma((8,)), dma, dma, dma((3,)), dma, dma((2,)),
            dma((8,)), dma((8,)), dma((12,)), dma((12,)), dma((3,)), dma((3,)),
        ],
        compiler_params=pltpu.CompilerParams(
            collective_id=0 if remote else None,
            has_side_effects=True,
            vmem_limit_bytes=56 * 2**20,
        ),
        cost_estimate=pl.CostEstimate(
            flops=2 * 10**9, bytes_accessed=18 * 10**6, transcendentals=0
        ),
    )(*args)


def on_device(zvecs, coef, blocks, send_idx, land_idx, active, order):
    strips, mask = assemble_call(True, zvecs, coef, blocks, send_idx, land_idx, active, order)
    return pl.pallas_call(
        place_strips,
        out_shape=jax.ShapeDtypeStruct((NCOL * K, WIDE), f32),
        in_specs=[pl.BlockSpec(memory_space=pltpu.VMEM)] * 2,
        out_specs=pl.BlockSpec(memory_space=pltpu.VMEM),
    )(strips, mask)


def solution(mesh):
    in_specs = (
        P("row", "col", None, None, None),
        P("row", "col", None, None),
        P("row", "col", None, None, None),
        P("row", "col", None, None),
        P("row", "col", None, None),
        P("row", "col", None),
        P(),
    )
    return jax.shard_map(
        on_device, mesh=mesh, in_specs=in_specs, out_specs=P("row", "col"), check_vma=False
    )
```
